512 devices in a mesh: place: 16 (over y, x_hi, core), tok: 32 (over z, x_lo).
Axes of the slice: x: 4 (x_hi: 2, x_lo: 2; x = x_hi * 2 + x_lo), y: 4, z: 16, core: 2. Of those that a mesh axis runs over, the one named last changes fastest.
Arguments:
- tokens: bfloat16 [8192, 2048], P('tok', 'place'), may hold values from -6 to 6
- mod_shift: float32 [2048], replicated, may hold values from -3 to 3
- mod_scale: float32 [2048], replicated, may hold values from -2.5 to 2.5
- res_gate: float32 [2048], replicated, may hold values from 0.5 to 1.5
- weight_in: bfloat16 [32, 2048, 8192], P('tok', None, 'place'), may hold values from -0.125 to 0.125
- weight_out: bfloat16 [32, 8192, 2048], P('tok', 'place'), may hold values from -0.09375 to 0.09375
- expert_slot: int32 [32], replicated, may hold values from 0 to 31, each once
- routes: int32 [8192, 2], P('tok'), may hold values from 0 to 31, all different within a row; in each aligned block of 256 rows (0 to 255, 256 to 511, ...) at most 24 rows name the same one
- gate_fixed: int32 [8192, 2], P('tok'), may hold values from 1 to 65535
Outputs:
- mixed: bfloat16 [8192, 2048], P('tok', 'place')
The draws below stay inside these ranges and needn't reach their ends.
Inputs may be any that keep to these rules, and one draw needn't show every extreme that they name: `routes`: among the 256 tokens of one index of tok (aligned blocks of rows), no expert is named by more than 24 rows, a bound that some block reaches; each row names two different experts. A permutation: expert e's weights are slot expert_slot[e] of weight_in and weight_out.
All inputs are finite; a program needn't handle non-finite values.
Results may differ from the reference program's by a relative error of at most 0.013.
Values may be sent and summed in bfloat16 or wider, within the bound.
A program may use at most 64 MiB of HBM per device.

```python
import math
import jax
import jax.numpy as jnp
import numpy as np
from jax import lax

D = 2048
FF = 8192
EXPERTS = 32
TOK_DEV = 256
CAP = 24
TOKENS = 8192
N_PLACE = 16
N_TOK = 32


def set_ends(array, key, low, high):
    dims = array.shape
    index_at = [jax.random.randint(jax.random.fold_in(key, axis), (), 0, dims[axis]) for axis in range(len(dims))]
    array = array.at[tuple(index_at)].set(low)
    longest = dims.index(max(dims))
    index_at[longest] = (index_at[longest] + 1) % dims[longest]
    return array.at[tuple(index_at)].set(high)


def with_spikes(result, key, source, target, blocks, factor):
    def block_of(axis_at):
        return (jnp.arange(result.shape[axis_at]) // (result.shape[axis_at] // blocks)).reshape((-1,) + (1,) * (result.ndim - 1 - axis_at))

    one_side = jax.random.permutation(key, blocks)[block_of(target)]
    second = (block_of(target) + blocks // 2) % blocks
    return jnp.where((block_of(source) == one_side) | (block_of(source) == second), factor * result, result)


def level_of(stream_key, shape, shards, low, high):
    factor_of = 1.0
    for dim, parts in shards:
        draws = jax.random.uniform(jax.random.fold_in(jax.random.fold_in(stream_key, 6), dim), (parts,), jnp.float32, low / len(shards), high / len(shards))
        factor_of = factor_of * jnp.repeat(jnp.exp(draws), shape[dim] // parts).reshape((-1,) + (1,) * (len(shape) - 1 - dim))
    return factor_of


def assign_block(stream_key, own, number, rows, amount, top, bound, lean):
    ranking = jax.random.permutation(stream_key, amount)
    heavy_load, ordinary = load_shares(amount, rows * top, bound, lean, True), load_shares(amount, rows * top, bound, lean, False)
    places = jnp.arange(amount)

    def named(tallies, rotation):
        used = int((tallies > 0).sum())
        fixed = max(1, used // 4)
        moved = fixed + (places - fixed + rotation * (used - fixed)) % max(1, amount - fixed)
        return jnp.zeros((amount,), jnp.int32).at[ranking[jnp.where(places < fixed, places, moved)]].set(jnp.asarray(tallies, jnp.int32))

    tallies = jnp.where(number % 4 == 0, named(heavy_load, number // 4), named(ordinary, number - number // 4 - 1))
    mixed = jax.random.permutation(jax.random.fold_in(own, 3), amount)
    giver, receiver = mixed[0:amount // 2 * 2:2], mixed[1:amount // 2 * 2:2]
    slack = jnp.minimum(tallies[giver] - 1, bound - tallies[receiver]) // 2
    slack = jnp.where((giver == ranking[0]) | (receiver == ranking[0]) | (tallies[receiver] == 0), 0, jnp.maximum(slack, 0))
    moved = jax.random.randint(jax.random.fold_in(own, 4), (amount // 2,), 0, 1 << 20) % (slack + 1)
    tallies = tallies.at[giver].add(-moved).at[receiver].add(moved)
    labels = jnp.searchsorted(jnp.cumsum(tallies), jnp.arange(rows * top), side="right").astype(jnp.int32)
    listing = labels.reshape(top, rows).T
    listing = listing[jax.random.permutation(jax.random.fold_in(own, 1), rows)]
    rotation = jax.random.randint(jax.random.fold_in(own, 2), (rows, 1), 0, top)
    return jnp.take_along_axis(listing, (jnp.arange(top)[None, :] + rotation) % top, axis=1)


def load_shares(amount, total, bound, lean, full):
    weights = [(1 << 20) // math.isqrt(rank ** lean) + 1 for rank in range(1, amount + 1)]
    largest = bound if full else min(bound, max(-(-total // amount), total * weights[0] // sum(weights)))
    least = 1 if total - largest >= amount - 1 else 0
    counts, spare = [largest] + [least] * (amount - 1), total - largest - least * (amount - 1)
    while spare > 0:
        movable = [i for i in range(1, amount) if counts[i] < largest] or [i for i in range(1, amount) if counts[i] < bound]
        pool, remaining = sum([weights[i] for i in movable]), spare
        for i in movable:
            extra = min(bound - counts[i], max(1, remaining * weights[i] // pool), spare)
            counts[i] = counts[i] + extra
            spare = spare - extra
    return np.array(counts)


def noise(key, extent, spread, most, shards=(), kind=jnp.bfloat16):
    result = spread * jax.random.normal(key, extent, jnp.float32)
    if shards:
        result = result * level_of(key, extent, shards, -0.22, 0.18)
    return jnp.clip(result, -most, most).astype(kind)


def heavy_noise(rng, dims, scale, bound, cuts, heavy, kind=jnp.bfloat16):
    result = scale * jax.random.normal(rng, dims, jnp.float32)
    if cuts:
        result = result * level_of(rng, dims, cuts, -0.22, 0.18)
    return jnp.clip(with_spikes(result, jax.random.fold_in(rng, 3), *heavy), -bound, bound).astype(kind)


def setup_inputs(seed: int = 0) -> dict:
    arg_keys = jax.random.split(jax.random.key(seed), 10)
    tokens = noise(arg_keys[0], (TOKENS, D), 1.0, 6.0, ((0, 32), (1, 16)))
    mod_shift = noise(arg_keys[1], (D,), 0.5, 3.0, (), jnp.float32)
    mod_scale = noise(arg_keys[2], (D,), 0.3, 2.5, (), jnp.float32)
    res_gate = jnp.clip(jax.random.uniform(arg_keys[3], (D,), jnp.float32, 0.5, 1.5), 0.5, 1.5)
    weight_in = noise(arg_keys[4], (EXPERTS, D, FF), D ** -0.5, 0.125, ((0, 32), (2, 16)))
    weight_out = heavy_noise(arg_keys[5], (EXPERTS, FF, D), FF ** -0.5, 0.09375, ((0, 32), (1, 16)), (1, 2, 16, 2.0))
    expert_slot = jax.random.permutation(arg_keys[6], EXPERTS).astype(jnp.int32)
    routes_keys = jax.random.split(jax.random.fold_in(arg_keys[7], 1), TOKENS // TOK_DEV)
    routes_turns = jax.random.permutation(jax.random.fold_in(arg_keys[7], 3), TOKENS // TOK_DEV)
    routes = jax.vmap(lambda own, number: assign_block(jax.random.fold_in(arg_keys[7], 2), own, number, TOK_DEV, EXPERTS, 2, CAP, 2))(routes_keys, routes_turns).reshape((TOKENS, 2))
    gate_fixed = set_ends(jax.random.randint(arg_keys[8], (TOKENS, 2), 1, 65536), jax.random.fold_in(arg_keys[8], 1), 1, 65535).astype(jnp.int32)
    return dict(tokens=tokens, mod_shift=mod_shift, mod_scale=mod_scale, res_gate=res_gate, weight_in=weight_in, weight_out=weight_out, expert_slot=expert_slot, routes=routes, gate_fixed=gate_fixed)


def reference(tokens, mod_shift, mod_scale, res_gate, weight_in, weight_out, expert_slot, routes, gate_fixed):
    as_float = tokens.astype(jnp.float32)
    row_mean = lax.optimization_barrier(jnp.mean(as_float, axis=1, keepdims=True))
    row_square = lax.optimization_barrier(jnp.mean(as_float * as_float, axis=1, keepdims=True))
    inverse = lax.rsqrt(row_square - row_mean * row_mean + 1e-06)
    normed = ((as_float - row_mean) * inverse * (1.0 + mod_scale[None, :]) + mod_shift[None, :]).astype(jnp.bfloat16)
    gate_values = gate_fixed.astype(jnp.float32).reshape(-1) / 65536.0
    flat_routes = routes.reshape(-1).astype(jnp.int32)
    limit = N_TOK * CAP
    block_size = FF // N_PLACE

    def one_expert(running, expert):
        matches = flat_routes == expert
        chosen = jnp.nonzero(matches, size=limit, fill_value=0)[0].astype(jnp.int32)
        counted = jnp.sum(matches.astype(jnp.int32))
        valid = jnp.arange(limit, dtype=jnp.int32) < counted
        token_index = chosen // 2
        picked = normed[token_index]
        slot_index = expert_slot[expert]
        first_proj = weight_in[slot_index]
        second_proj = weight_out[slot_index]
        hidden = jax.nn.gelu(jnp.dot(picked, first_proj, preferred_element_type=jnp.float32), approximate=True).astype(jnp.bfloat16)
        blocks = jnp.einsum('rjf,jfd->jrd', hidden.reshape(limit, N_PLACE, block_size).astype(jnp.float32), second_proj.reshape(N_PLACE, block_size, D).astype(jnp.float32), precision=lax.Precision.HIGHEST)
        blocks = lax.optimization_barrier(blocks.astype(jnp.bfloat16)).astype(jnp.float32)
        expert_out = lax.optimization_barrier(lax.optimization_barrier(jnp.sum(blocks, axis=0)).astype(jnp.bfloat16)).astype(jnp.float32)
        weighting = jnp.where(valid, gate_values[chosen], jnp.float32(0.0))
        running = running.at[token_index].add(weighting[:, None] * expert_out)
        return (running, None)
    combined, _ = lax.scan(one_expert, jnp.zeros(tokens.shape, jnp.float32), jnp.arange(EXPERTS, dtype=jnp.int32))
    return (as_float + res_gate[None, :] * combined).astype(jnp.bfloat16)
```

```python
import functools

import jax
import jax.numpy as jnp
from jax import lax
from jax.experimental import pallas as pl
from jax.experimental.pallas import tpu as pltpu
from jax.sharding import PartitionSpec as P

D = 2048
CAP = 24
CHUNKS = 1
CHIPS = 8
PLACES = 16
LANES = 128
WIDE = 256
MESH = pl.DeviceIdType.MESH
F32 = jnp.float32
BF16 = jnp.bfloat16


def remote(src, dst, send_sem, recv_sem, device):
    return pltpu.make_async_remote_copy(
        src_ref=src,
        dst_ref=dst,
        send_sem=send_sem,
        recv_sem=recv_sem,
        device_id=device,
        device_id_type=MESH,
    )


def to_rows(block):
    slots = block.shape[0]
    wide = block.astype(F32)
    halves = [wide[:, h * CAP : (h + 1) * CAP].reshape(slots * CAP, LANES) for h in range(2)]
    return jnp.concatenate(halves, axis=1).astype(BF16)


def to_messages(rows):
    slots = rows.shape[0] // CAP
    halves = [rows[:, h * LANES : (h + 1) * LANES].reshape(slots, CAP, LANES) for h in range(2)]
    return jnp.concatenate(halves, axis=1).astype(BF16)


def kernel(
    n_tok,
    tokens,
    shift,
    scale,
    gate,
    routes,
    fixed,
    catalog,
    w_in,
    w_out,
    out,
    tok2,
    stat_out,
    stat_in,
    sent_rows,
    got_rows,
    held,
    win,
    wout,
    hid,
    part_own,
    part_near,
    far_out,
    far_in,
    near_out,
    near_in,
    x_out,
    x_in,
    back_out,
    back_in,
    pick_hi,
    pick_lo,
    comb,
    comb_in,
    w_sem,
    one_send,
    one_recv,
    stat_send,
    stat_recv,
    disp_send,
    disp_recv,
    gat_send,
    gat_recv,
    red_send,
    red_recv,
    back_send,
    back_recv,
):
    place, tok = lax.axis_index("place"), lax.axis_index("tok")
    nz = n_tok // 2
    slots_chunk = nz // CHUNKS
    rows = slots_chunk * CAP
    half = rows // 2
    core, chip = lax.rem(place, 2), lax.div(place, 2)
    xh, y = lax.rem(chip, 2), lax.div(chip, 2)
    z, xl = lax.div(tok, 2), lax.rem(tok, 2)
    sibling = (place + 1 - 2 * core, tok)
    across = (place + 2 - 4 * xh, tok)
    y_right, y_left, y_far = lax.rem(y + 1, 4), lax.rem(y + 3, 4), lax.rem(y + 2, 4)
    right = (y_right * 4 + xh * 2 + core, tok)
    left = (y_left * 4 + xh * 2 + core, tok)

    def mate(offset):
        return (lax.rem(place + offset, PLACES), tok)

    def peer(dz):
        return (place, lax.rem(z + dz, nz) * 2 + lax.rem(xl + core, 2))

    def step_of(d):
        return jnp.where(lax.rem(d, 2) == 1, lax.div(d + 1, 2), lax.rem(nz - lax.div(d, 2), nz))

    def piece(y_of, a):
        return y_of * 2 + lax.rem(xh + 1 + a, 2)

    barrier = pltpu.get_barrier_semaphore()

    def greet_place(offset, carry):
        pl.semaphore_signal(barrier, inc=1, device_id=mate(offset), device_id_type=MESH)
        return carry

    def greet_tok(dz, carry):
        pl.semaphore_signal(barrier, inc=1, device_id=peer(dz), device_id_type=MESH)
        return carry

    lax.fori_loop(1, PLACES, greet_place, 0)
    lax.fori_loop(1, nz, greet_tok, 0)

    @pl.when(core == 1)
    def _():
        greet_tok(0, 0)

    load_in = pltpu.make_async_copy(w_in.at[0], win.at[core], w_sem.at[0])
    load_out = pltpu.make_async_copy(w_out.at[0], wout.at[core], w_sem.at[1])
    load_in.start()
    load_out.start()

    count = tokens.shape[0]
    eye = lax.broadcasted_iota(jnp.int32, (count, count), 0) == lax.broadcasted_iota(
        jnp.int32, (count, count), 1
    )

    def as_row(column):
        return jnp.sum(jnp.where(eye, column, 0.0), axis=0, keepdims=True)

    def as_column(row):
        return jnp.sum(jnp.where(eye, row, 0.0), axis=1, keepdims=True)

    own = tokens[...].astype(F32)
    total_row = as_row(jnp.sum(own, axis=1, keepdims=True))
    square_row = as_row(jnp.sum(own * own, axis=1, keepdims=True))
    lines = lax.broadcasted_iota(jnp.int32, (8, count), 0)
    stat_out[...] = jnp.where(lines == 0, total_row, jnp.where(lines == 1, square_row, 0.0))
    tok2[core] = tokens[...]

    pl.semaphore_wait(barrier, PLACES - 1 + nz - 1 + core)

    def stat_copy(offset):
        return remote(
            stat_out, stat_in.at[offset], stat_send.at[offset], stat_recv.at[offset], mate(offset)
        )

    def start_stat(offset, carry):
        stat_copy(offset).start()
        return carry

    lax.fori_loop(1, PLACES, start_stat, 0)
    tok_copy = remote(tokens, tok2.at[core], one_send.at[0], one_recv.at[0], sibling)
    tok_copy.start()
    win_copy = remote(w_in.at[0], win.at[core], one_send.at[1], one_recv.at[1], sibling)
    wout_copy = remote(w_out.at[0], wout.at[core], one_send.at[2], one_recv.at[2], sibling)
    win_copy.start()
    wout_copy.start()

    experts = catalog.shape[1]
    kinds = lax.broadcasted_iota(jnp.int32, (experts, count), 0)
    small_eye = lax.broadcasted_iota(jnp.int32, (experts, experts), 0) == lax.broadcasted_iota(
        jnp.int32, (experts, experts), 1
    )
    slot_column = jnp.sum(
        jnp.where(small_eye, catalog[...].astype(F32), 0.0), axis=1, keepdims=True
    )
    hot = [kinds == routes[k : k + 1, :] for k in range(2)]
    ones = [jnp.where(h, 1.0, 0.0) for h in hot]
    before = (
        lax.broadcasted_iota(jnp.int32, (count, count), 0)
        < lax.broadcasted_iota(jnp.int32, (count, count), 1)
    )
    earlier = jnp.dot(
        (ones[0] + ones[1]).astype(BF16),
        jnp.where(before, 1.0, 0.0).astype(BF16),
        preferred_element_type=F32,
    )
    target = []
    for k in range(2):
        position = jnp.sum(ones[k] * earlier, axis=0, keepdims=True).astype(jnp.int32)
        slot = jnp.sum(ones[k] * slot_column, axis=0, keepdims=True).astype(jnp.int32)
        dz = jnp.bitwise_and((slot >> 1) - z + nz, nz - 1)
        order = jnp.where(dz == 0, 0, jnp.where(2 * dz <= nz, 2 * dz - 1, 2 * (nz - dz)))
        mine = jnp.bitwise_and(slot + xl, 1) == core
        target.append(jnp.where(mine, order * CAP + position, -1))
    every = lax.broadcasted_iota(jnp.int32, (nz * CAP, count), 0)
    pick = jnp.where((every == target[0]) | (every == target[1]), 1.0, 0.0).astype(BF16)

    column = [as_column(t.astype(F32)) for t in target]
    high, low = [], []
    for k in range(2):
        value = fixed[k : k + 1, :]
        high.append(as_column((value >> 8).astype(F32)))
        low.append(as_column(jnp.bitwise_and(value, 255).astype(F32)))
    for k in range(CHUNKS):
        lane = (lax.broadcasted_iota(jnp.int32, (count, rows), 1) + k * rows).astype(F32)
        for ref, part in ((pick_hi, high), (pick_lo, low)):
            ref[k] = (
                jnp.where(lane == column[0], part[0], 0.0)
                + jnp.where(lane == column[1], part[1], 0.0)
            ).astype(BF16)

    def wait_stat(offset, carry):
        stat_copy(offset).wait_recv()
        return carry + stat_in[offset]

    sums = lax.fori_loop(1, PLACES, wait_stat, stat_out[...])
    mean_row = sums[0:1, :] / D
    inverse_row = lax.rsqrt(sums[1:2, :] / D - mean_row * mean_row + 1e-06)
    mean, inverse = as_column(mean_row), as_column(inverse_row)
    remote(tokens, tok2.at[1 - core], one_send.at[0], one_recv.at[0], sibling).wait_recv()
    both = jnp.concatenate([tok2[0], tok2[1]], axis=1).astype(F32)
    lanes = pl.ds(pl.multiple_of(chip * WIDE, WIDE), WIDE)
    normed = ((both - mean) * inverse * (1.0 + scale[:, lanes]) + shift[:, lanes]).astype(BF16)
    sent_rows[...] = to_messages(jnp.dot(pick, normed, preferred_element_type=F32))

    def disp_copy(d):
        return remote(
            sent_rows.at[d], got_rows.at[d], disp_send.at[d], disp_recv.at[d], peer(step_of(d))
        )

    def start_disp(d, carry):
        disp_copy(d).start()
        return carry

    @pl.when(core == 1)
    def _():
        disp_copy(0).start()

    lax.fori_loop(1, nz, start_disp, 0)

    @pl.when(core == 0)
    def _():
        got_rows[0] = sent_rows[0]

    waits = []

    def go(copy):
        copy.start()
        waits.append(copy)

    def wait_disp(d, carry):
        disp_copy(d).wait_recv()
        return carry

    def gather_start(k):
        lo = k * slots_chunk
        if k == 0:
            @pl.when(core == 1)
            def _():
                disp_copy(0).wait_recv()

        lax.fori_loop(max(lo, 1), lo + slots_chunk, wait_disp, 0)
        held[k, chip] = to_rows(got_rows[lo : lo + slots_chunk])
        mine = held.at[k, chip]
        go(remote(mine, mine, gat_send.at[k, 0], gat_recv.at[k, 0], across))
        go(remote(mine, mine, gat_send.at[k, 1], gat_recv.at[k, 1], right))
        go(remote(mine, mine, gat_send.at[k, 2], gat_recv.at[k, 2], left))

    def arrived(k, i, ref):
        remote(ref, ref, gat_send.at[k, i], gat_recv.at[k, i], across).wait_recv()

    def gather_across(k):
        other = held.at[k, piece(y, 0)]
        arrived(k, 0, other)
        go(remote(other, other, gat_send.at[k, 3], gat_recv.at[k, 3], right))
        go(remote(other, other, gat_send.at[k, 4], gat_recv.at[k, 4], left))

    def gather_pass(k, a):
        base = 1 + 2 * (1 - a)
        from_left, from_right = held.at[k, piece(y_left, a)], held.at[k, piece(y_right, a)]
        first, second = pl.ds(0, half), pl.ds(half, half)
        arrived(k, base, from_left)
        ref = from_left.at[first]
        go(remote(ref, ref, gat_send.at[k, base + 4], gat_recv.at[k, base + 4], right))
        arrived(k, base + 1, from_right)
        ref = from_right.at[second]
        go(remote(ref, ref, gat_send.at[k, base + 5], gat_recv.at[k, base + 5], left))

    def gather_end(k, a):
        base = 5 + 2 * (1 - a)
        far = held.at[k, piece(y_far, a)]
        arrived(k, base, far.at[pl.ds(0, half)])
        arrived(k, base + 1, far.at[pl.ds(half, half)])

    tiles = win.shape[2] // WIDE

    def hidden(k):
        x = jnp.concatenate([held[k, q] for q in range(CHIPS)], axis=1)
        for c in range(2):
            for t in range(tiles):
                h = jnp.dot(
                    x, win[c, :, t * WIDE : (t + 1) * WIDE], preferred_element_type=F32
                )
                hid[c, :, t * WIDE : (t + 1) * WIDE] = jax.nn.gelu(h, approximate=True).astype(BF16)

    def second(q):
        lanes_q = pl.ds(pl.multiple_of(q * WIDE, WIDE), WIDE)
        return jnp.dot(hid[0], wout[0, :, lanes_q], preferred_element_type=F32) + jnp.dot(
            hid[1], wout[1, :, lanes_q], preferred_element_type=F32
        )

    def landed(k, i, ref):
        remote(ref, ref, red_send.at[k, i], red_recv.at[k, i], across).wait_recv()

    def reduce_start(k):
        for a in range(2):
            far_out[k, a] = second(piece(y_far, a)).astype(BF16)
            for i, to in ((0, right), (1, left)):
                src = far_out.at[k, a, pl.ds(i * half, half)]
                dst = far_in.at[k, a, pl.ds(i * half, half)]
                go(remote(src, dst, red_send.at[k, 2 * i + a], red_recv.at[k, 2 * i + a], to))
        for a in range(2):
            part_near[a, 0] = second(piece(y_right, a))
            part_near[a, 1] = second(piece(y_left, a))
        for a in range(2):
            part_own[k, a] = second(piece(y, a))

    def reduce_near(k, a):
        for i, to in ((0, right), (1, left)):
            here = pl.ds(i * half, half)
            rest = pl.ds((1 - i) * half, half)
            landed(k, 2 * i + a, far_in.at[k, a, here])
            near_out[k, a, i, here] = (
                part_near[a, i, here] + far_in[k, a, here].astype(F32)
            ).astype(BF16)
            near_out[k, a, i, rest] = part_near[a, i, rest].astype(BF16)
            j = 4 + 2 * i + a
            go(
                remote(
                    near_out.at[k, a, i], near_in.at[k, a, i], red_send.at[k, j], red_recv.at[k, j], to
                )
            )

    def reduce_own(k, a):
        total = part_own[k, a]
        for i in range(2):
            landed(k, 4 + 2 * i + a, near_in.at[k, a, i])
            total = total + near_in[k, a, i].astype(F32)
        return total

    def reduce_across(k):
        x_out[k] = reduce_own(k, 0).astype(BF16)
        go(remote(x_out.at[k], x_in.at[k], red_send.at[k, 8], red_recv.at[k, 8], across))

    def back_copy(d):
        return remote(
            back_out.at[d], back_in.at[d], back_send.at[d], back_recv.at[d], peer(nz - step_of(d))
        )

    def start_back(d, carry):
        back_copy(d).start()
        return carry

    def wait_back(d, carry):
        back_copy(d).wait_recv()
        return carry

    def give_back(k):
        mine = reduce_own(k, 1)
        landed(k, 8, x_in.at[k])
        lo = k * slots_chunk
        back_out[lo : lo + slots_chunk] = to_messages(mine + x_in[k].astype(F32))
        if k == 0:
            @pl.when(core == 1)
            def _():
                back_copy(0).start()

            @pl.when(core == 0)
            def _():
                back_in[0] = back_out[0]

        lax.fori_loop(max(lo, 1), lo + slots_chunk, start_back, 0)

    def combine(k):
        lo = k * slots_chunk
        if k == 0:
            @pl.when(core == 1)
            def _():
                back_copy(0).wait_recv()

        lax.fori_loop(max(lo, 1), lo + slots_chunk, wait_back, 0)
        values = to_rows(back_in[lo : lo + slots_chunk])
        return 256.0 * jnp.dot(pick_hi[k], values, preferred_element_type=F32) + jnp.dot(
            pick_lo[k], values, preferred_element_type=F32
        )

    for k in range(CHUNKS):
        gather_start(k)
    for k in range(CHUNKS):
        gather_across(k)
    for k in range(CHUNKS):
        gather_pass(k, 1)
    for k in range(CHUNKS):
        gather_pass(k, 0)
    load_in.wait()
    load_out.wait()
    remote(w_in.at[0], win.at[1 - core], one_send.at[1], one_recv.at[1], sibling).wait_recv()
    remote(w_out.at[0], wout.at[1 - core], one_send.at[2], one_recv.at[2], sibling).wait_recv()
    for k in range(CHUNKS):
        gather_end(k, 1)
        gather_end(k, 0)
        hidden(k)
        reduce_start(k)
        for a in range(2):
            reduce_near(k, a)
        reduce_across(k)
        give_back(k)
    answer = combine(0)
    for k in range(1, CHUNKS):
        answer = answer + combine(k)
    answer = answer / 65536.0
    comb[0] = answer[:, :LANES]
    comb[1] = answer[:, LANES:]
    comb_copy = remote(comb.at[1 - core], comb_in, one_send.at[3], one_recv.at[3], sibling)
    comb_copy.start()
    comb_copy.wait_recv()
    my_lanes = pl.ds(pl.multiple_of(place * LANES, LANES), LANES)
    out[...] = (
        tokens[...].astype(F32) + gate[:, my_lanes] * (comb[core] + comb_in[...])
    ).astype(BF16)

    comb_copy.wait_send()
    tok_copy.wait_send()
    win_copy.wait_send()
    wout_copy.wait_send()
    for copy in waits:
        copy.wait_send()

    def left_stat(offset, carry):
        stat_copy(offset).wait_send()
        return carry

    def left_rows(d, carry):
        disp_copy(d).wait_send()
        back_copy(d).wait_send()
        return carry

    lax.fori_loop(1, PLACES, left_stat, 0)
    lax.fori_loop(1, nz, left_rows, 0)

    @pl.when(core == 1)
    def _():
        left_rows(0, 0)


def shards(
    tokens, mod_shift, mod_scale, res_gate, weight_in, weight_out, expert_slot, routes, gate_fixed
):
    n_tok = lax.axis_size("tok")
    nz = n_tok // 2
    count = tokens.shape[0]
    units = weight_in.shape[2]
    rows = nz // CHUNKS * CAP
    vmem = pl.BlockSpec(memory_space=pltpu.VMEM)
    anywhere = pl.BlockSpec(memory_space=pl.ANY)
    dma = pltpu.SemaphoreType.DMA
    scratch = [
        pltpu.VMEM((2, count, LANES), BF16),
        pltpu.VMEM((8, count), F32),
        pltpu.VMEM((PLACES, 8, count), F32),
        pltpu.VMEM((nz, 2 * CAP, LANES), BF16),
        pltpu.VMEM((nz, 2 * CAP, LANES), BF16),
        pltpu.VMEM((CHUNKS, CHIPS, rows, WIDE), BF16),
        pltpu.VMEM((2, D, units), BF16),
        pltpu.VMEM((2, units, D), BF16),
        pltpu.VMEM((2, rows, units), BF16),
        pltpu.VMEM((CHUNKS, 2, rows, WIDE), F32),
        pltpu.VMEM((2, 2, rows, WIDE), F32),
        pltpu.VMEM((CHUNKS, 2, rows, WIDE), BF16),
        pltpu.VMEM((CHUNKS, 2, rows, WIDE), BF16),
        pltpu.VMEM((CHUNKS, 2, 2, rows, WIDE), BF16),
        pltpu.VMEM((CHUNKS, 2, 2, rows, WIDE), BF16),
        pltpu.VMEM((CHUNKS, rows, WIDE), BF16),
        pltpu.VMEM((CHUNKS, rows, WIDE), BF16),
        pltpu.VMEM((nz, 2 * CAP, LANES), BF16),
        pltpu.VMEM((nz, 2 * CAP, LANES), BF16),
        pltpu.VMEM((CHUNKS, count, rows), BF16),
        pltpu.VMEM((CHUNKS, count, rows), BF16),
        pltpu.VMEM((2, count, LANES), F32),
        pltpu.VMEM((count, LANES), F32),
        dma((2,)),
        dma((4,)),
        dma((4,)),
        dma((PLACES,)),
        dma((PLACES,)),
        dma((nz,)),
        dma((nz,)),
        dma((CHUNKS, 9)),
        dma((CHUNKS, 9)),
        dma((CHUNKS, 9)),
        dma((CHUNKS, 9)),
        dma((nz,)),
        dma((nz,)),
    ]
    return pl.pallas_call(
        functools.partial(kernel, n_tok),
        out_shape=jax.ShapeDtypeStruct(tokens.shape, BF16),
        in_specs=[vmem] * 7 + [anywhere] * 2,
        out_specs=vmem,
        scratch_shapes=scratch,
        compiler_params=pltpu.CompilerParams(
            collective_id=0, has_side_effects=True, vmem_limit_bytes=48 * 1024 * 1024
        ),
        cost_estimate=pl.CostEstimate(
            flops=4 * 2 * rows * CHUNKS * D * units,
            bytes_accessed=4 * D * units,
            transcendentals=2 * rows * CHUNKS * units,
        ),
    )(
        tokens,
        mod_shift[None, :],
        mod_scale[None, :],
        res_gate[None, :],
        routes.T,
        gate_fixed.T,
        expert_slot[None, :],
        weight_in,
        weight_out,
    )


def solution(mesh):
    placed = (
        P("tok", "place"),
        P(),
        P(),
        P(),
        P("tok", None, "place"),
        P("tok", "place", None),
        P(),
        P("tok", None),
        P("tok", None),
    )
    return jax.shard_map(
        shards, mesh=mesh, in_specs=placed, out_specs=P("tok", "place"), check_vma=False
    )
```

```python
import functools

import jax
import jax.numpy as jnp
from jax import lax
from jax.experimental import pallas as pl
from jax.experimental.pallas import tpu as pltpu
from jax.sharding import PartitionSpec as P

D = 2048
CAP = 24
CHUNKS = 4
STEPS = (0, 1, 15, 2, 14, 3, 13, 4, 12, 5, 11, 6, 10, 7, 9, 8)
GATHER = "DBDD"
REDUCE = "ADDD"
ORDER = (
    ("A", 0), ("A", 1), ("A", 2), ("H", 0), ("F1L", 1), ("F1R", 1), ("A", 3), ("S0", 0), ("S1", 0),
    ("SN", 0), ("SO", 0), ("H", 2), ("G", 1), ("S", 2), ("SO", 2), ("N0R", 0), ("N0L", 0), ("N1R", 0),
    ("N1L", 0), ("H", 3), ("S", 3), ("SO", 3), ("H", 1), ("S", 1), ("O0", 0), ("SO", 1), ("O1", 2),
    ("O1", 3), ("C", 2), ("O1", 1), ("O1", 0), ("C", 3), ("C", 1), ("C", 0),
)
CHIPS = 8
PLACES = 16
LANES = 128
WIDE = 256
MESH = pl.DeviceIdType.MESH
F32 = jnp.float32
BF16 = jnp.bfloat16


def remote(src, dst, send_sem, recv_sem, device):
    return pltpu.make_async_remote_copy(
        src_ref=src,
        dst_ref=dst,
        send_sem=send_sem,
        recv_sem=recv_sem,
        device_id=device,
        device_id_type=MESH,
    )


def to_rows(block):
    slots = block.shape[0]
    wide = block.astype(F32)
    halves = [wide[:, h * CAP : (h + 1) * CAP].reshape(slots * CAP, LANES) for h in range(2)]
    return jnp.concatenate(halves, axis=1).astype(BF16)


def to_messages(rows):
    slots = rows.shape[0] // CAP
    halves = [rows[:, h * LANES : (h + 1) * LANES].reshape(slots, CAP, LANES) for h in range(2)]
    return jnp.concatenate(halves, axis=1).astype(BF16)


def kernel(
    n_tok,
    tokens_hbm,
    shift_hbm,
    scale_hbm,
    gate_hbm,
    routes_hbm,
    fixed_hbm,
    catalog_hbm,
    w_in,
    w_out,
    out,
    shift,
    scale,
    gate,
    routes,
    fixed,
    catalog,
    tok2,
    sent_rows,
    got_rows,
    held,
    normed,
    win,
    wout,
    hid,
    part_own,
    part_near,
    far_out,
    far_in,
    near_out,
    near_in,
    x_out,
    x_in,
    back_out,
    back_in,
    pick_hi,
    pick_lo,
    total,
    comb,
    comb_in,
    w_sem,
    one_send,
    one_recv,
    disp_send,
    disp_recv,
    gat_send,
    gat_recv,
    red_send,
    red_recv,
    back_send,
    back_recv,
):
    place, tok = lax.axis_index("place"), lax.axis_index("tok")
    nz = n_tok // 2
    steps = STEPS[:nz]
    slots_chunk = nz // CHUNKS
    rows = slots_chunk * CAP
    half = rows // 2
    first, second = pl.ds(0, half), pl.ds(half, half)
    core, chip = lax.rem(place, 2), lax.div(place, 2)
    xh, y = lax.rem(chip, 2), lax.div(chip, 2)
    z, xl = lax.div(tok, 2), lax.rem(tok, 2)
    sibling = (place + 1 - 2 * core, tok)
    across = (place + 2 - 4 * xh, tok)
    y_right, y_left, y_far = lax.rem(y + 1, 4), lax.rem(y + 3, 4), lax.rem(y + 2, 4)
    right = (y_right * 4 + xh * 2 + core, tok)
    left = (y_left * 4 + xh * 2 + core, tok)

    def mate(offset):
        return (lax.rem(place + 2 * offset, PLACES), tok)

    def peer(dz):
        return (place, lax.rem(z + dz, nz) * 2 + lax.rem(xl + core, 2))

    def piece(y_of, a):
        return y_of * 2 + lax.rem(xh + 1 + a, 2)

    barrier = pltpu.get_barrier_semaphore()

    def greet(device):
        pl.semaphore_signal(barrier, inc=1, device_id=device, device_id_type=MESH)

    for dz in steps[1:]:
        greet(peer(dz))

    @pl.when(core == 1)
    def _():
        greet(peer(0))

    for offset in range(1, CHIPS):
        greet(mate(offset))
    greet(sibling)

    lanes = pl.ds(pl.multiple_of(chip * WIDE, WIDE), WIDE)
    my_lanes = pl.ds(pl.multiple_of(place * LANES, LANES), LANES)
    pairs = (
        (routes_hbm, routes),
        (catalog_hbm, catalog),
        (tokens_hbm, tok2.at[core]),
        (fixed_hbm, fixed),
        (scale_hbm, scale),
        (shift_hbm, shift),
        (gate_hbm.at[:, my_lanes], gate),
        (w_in.at[0], win.at[core]),
        (w_out.at[0], wout.at[core]),
    )
    loads = [pltpu.make_async_copy(src, dst, w_sem.at[i]) for i, (src, dst) in enumerate(pairs)]
    for copy in loads:
        copy.start()

    loads[0].wait()
    loads[1].wait()
    count = tokens_hbm.shape[0]
    experts = catalog.shape[1]
    kinds = lax.broadcasted_iota(jnp.int32, (experts, count), 0)
    small_eye = lax.broadcasted_iota(jnp.int32, (experts, experts), 0) == lax.broadcasted_iota(
        jnp.int32, (experts, experts), 1
    )
    slot_column = jnp.sum(
        jnp.where(small_eye, catalog[...].astype(F32), 0.0), axis=1, keepdims=True
    )
    ones = [jnp.where(kinds == routes[k : k + 1, :], 1.0, 0.0) for k in range(2)]
    down = lax.broadcasted_iota(jnp.int32, (count, count), 0)
    along = lax.broadcasted_iota(jnp.int32, (count, count), 1)
    earlier = jnp.dot(
        (ones[0] + ones[1]).astype(BF16),
        jnp.where(down < along, 1.0, 0.0).astype(BF16),
        preferred_element_type=F32,
    )
    target = []
    for k in range(2):
        position = jnp.sum(ones[k] * earlier, axis=0, keepdims=True).astype(jnp.int32)
        slot = jnp.sum(ones[k] * slot_column, axis=0, keepdims=True).astype(jnp.int32)
        dz = jnp.bitwise_and((slot >> 1) - z + nz, nz - 1)
        order = jnp.zeros_like(dz)
        for d, step in enumerate(steps):
            order = jnp.where(dz == step, d, order)
        mine = jnp.bitwise_and(slot + xl, 1) == core
        target.append(jnp.where(mine, order * CAP + position, -1))
    every = lax.broadcasted_iota(jnp.int32, (nz * CAP, count), 0)
    pick = jnp.where((every == target[0]) | (every == target[1]), 1.0, 0.0).astype(BF16)

    pl.semaphore_wait(barrier, CHIPS + nz - 1 + core)
    tok_copy = remote(tokens_hbm, tok2.at[core], one_send.at[0], one_recv.at[0], sibling)
    win_copy = remote(w_in.at[0], win.at[core], one_send.at[1], one_recv.at[1], sibling)
    wout_copy = remote(w_out.at[0], wout.at[core], one_send.at[2], one_recv.at[2], sibling)
    tok_copy.start()
    loads[2].wait()
    remote(tokens_hbm, tok2.at[1 - core], one_send.at[0], one_recv.at[0], sibling).wait_recv()

    picked = jnp.dot(
        pick, jnp.concatenate([tok2[0], tok2[1]], axis=1), preferred_element_type=F32
    )
    sent_rows[...] = to_messages(picked)

    def disp_copy(d):
        return remote(
            sent_rows.at[d], got_rows.at[d], disp_send.at[d], disp_recv.at[d], peer(steps[d])
        )

    @pl.when(core == 1)
    def _():
        disp_copy(0).start()

    for d in range(1, nz):
        disp_copy(d).start()

    @pl.when(core == 0)
    def _():
        got_rows[0] = sent_rows[0]

    win_copy.start()
    wout_copy.start()
    for i in range(3, 7):
        loads[i].wait()

    def as_column(row):
        return jnp.sum(jnp.where(down == along, row, 0.0), axis=1, keepdims=True)

    column = [as_column(t.astype(F32)) for t in target]
    high, low = [], []
    for k in range(2):
        value = fixed[k : k + 1, :]
        high.append(as_column((value >> 8).astype(F32)))
        low.append(as_column(jnp.bitwise_and(value, 255).astype(F32)))
    for k in range(CHUNKS):
        lane = (lax.broadcasted_iota(jnp.int32, (count, rows), 1) + k * rows).astype(F32)
        for ref, part in ((pick_hi, high), (pick_lo, low)):
            ref[k] = (
                jnp.where(lane == column[0], part[0], 0.0)
                + jnp.where(lane == column[1], part[1], 0.0)
            ).astype(BF16)

    sends = []

    def gat(k, i, ref, to):
        copy = remote(ref, ref, gat_send.at[k, i], gat_recv.at[k, i], to)
        copy.start()
        sends.append(copy)

    def gat_wait(k, i, ref):
        remote(ref, ref, gat_send.at[k, i], gat_recv.at[k, i], across).wait_recv()

    def red(k, i, src, dst, to):
        copy = remote(src, dst, red_send.at[k, i], red_recv.at[k, i], to)
        copy.start()
        sends.append(copy)

    def red_wait(k, i, ref):
        remote(ref, ref, red_send.at[k, i], red_recv.at[k, i], across).wait_recv()

    def slots_of(k, act):
        for d in range(k * slots_chunk, (k + 1) * slots_chunk):
            if d == 0:
                pl.when(core == 1)(functools.partial(act, d))
            else:
                act(d)

    def arrive(k):
        slots_of(k, lambda d: disp_copy(d).wait_recv())
        held[k, chip] = to_rows(got_rows[k * slots_chunk : (k + 1) * slots_chunk])
        mine = held.at[k, chip]
        if GATHER[k] == "D":
            for offset in DIRECT:
                gat(k, offset - 1, mine, mate(offset))
        else:
            gat(k, 0, mine, across)
            gat(k, 1, mine, right)
            gat(k, 2, mine, left)

    def arrive_across(k):
        other = held.at[k, piece(y, 0)]
        gat_wait(k, 0, other)
        gat(k, 3, other, right)
        gat(k, 4, other, left)

    def pass_on(k, a, from_left):
        i = 1 + 2 * (1 - a) + (0 if from_left else 1)
        ref = held.at[k, piece(y_left if from_left else y_right, a)]
        gat_wait(k, i, ref)
        gat(k, i + 4, ref.at[first if from_left else second], right if from_left else left)
        if GATHER[k] == "B":
            gat(k, i + 2, ref, across)

    def far_across(k):
        far = held.at[k, piece(y_far, 1)]
        gat_wait(k, 5, far.at[first])
        gat_wait(k, 6, far.at[second])
        gat(k, 7, far, across)

    def all_there(k):
        if GATHER[k] == "D":
            for offset in range(1, CHIPS):
                gat_wait(k, offset - 1, held.at[k, lax.rem(chip + CHIPS - offset, CHIPS)])
        elif GATHER[k] == "B":
            gat_wait(k, 0, held.at[k, piece(y, 0)])
            gat_wait(k, 3, held.at[k, piece(y_left, 0)])
            gat_wait(k, 4, held.at[k, piece(y_right, 0)])
            gat_wait(k, 7, held.at[k, piece(y_far, 0)])
        else:
            for a in range(2):
                far = held.at[k, piece(y_far, a)]
                gat_wait(k, 7 - 2 * a, far.at[first])
                gat_wait(k, 8 - 2 * a, far.at[second])

    tiles = win.shape[2] // WIDE
    ready = []

    def hidden(k):
        all_there(k)
        sums = jnp.zeros((rows, WIDE), F32)
        squares = jnp.zeros((rows, WIDE), F32)
        for q in range(CHIPS):
            x = held[k, q].astype(F32)
            sums += x
            squares += x * x
        mean = jnp.sum(sums, axis=1, keepdims=True) / D
        inverse = lax.rsqrt(jnp.sum(squares, axis=1, keepdims=True) / D - mean * mean + 1e-06)
        for q in range(CHIPS):
            at = slice(q * WIDE, (q + 1) * WIDE)
            x = held[k, q].astype(F32)
            normed[:, at] = (
                (x - mean) * inverse * (1.0 + scale[:, at]) + shift[:, at]
            ).astype(BF16)
        if not ready:
            ready.append(k)
            loads[7].wait()
            loads[8].wait()
            for i, (src, dst) in ((1, (w_in, win)), (2, (w_out, wout))):
                remote(src.at[0], dst.at[1 - core], one_send.at[i], one_recv.at[i], sibling).wait_recv()
        for c in range(2):
            for t in range(tiles):
                at = slice(t * WIDE, (t + 1) * WIDE)
                h = jnp.dot(normed[...], win[c, :, at], preferred_element_type=F32)
                hid[c, :, at] = jax.nn.gelu(h, approximate=True).astype(BF16)

    def result(q):
        at = pl.ds(pl.multiple_of(q * WIDE, WIDE), WIDE)
        return jnp.dot(hid[0], wout[0, :, at], preferred_element_type=F32) + jnp.dot(
            hid[1], wout[1, :, at], preferred_element_type=F32
        )

    def far_results(k, a):
        far_out[k, a] = result(piece(y_far, a)).astype(BF16)
        for i, (part, to) in enumerate(((first, right), (second, left))):
            red(k, 2 * i + a, far_out.at[k, a, part], far_in.at[k, a, part], to)

    def near_results(k):
        for a in range(2):
            part_near[a, 0] = result(piece(y_right, a))
            part_near[a, 1] = result(piece(y_left, a))

    def own_results(k):
        if REDUCE[k] == "D":
            part_own[k, 1] = result(chip)
        else:
            for a in range(2):
                part_own[k, a] = result(piece(y, a))

    def near_sum(k, a, i):
        here, rest = (first, second) if i == 0 else (second, first)
        red_wait(k, 2 * i + a, far_in.at[k, a, here])
        near_out[k, a, i, here] = (
            part_near[a, i, here] + far_in[k, a, here].astype(F32)
        ).astype(BF16)
        near_out[k, a, i, rest] = part_near[a, i, rest].astype(BF16)
        j = 4 + 2 * i + a
        red(k, j, near_out.at[k, a, i], near_in.at[k, a, i], right if i == 0 else left)

    def own_sum(k, a):
        value = part_own[k, a]
        for i in range(2):
            red_wait(k, 4 + 2 * i + a, near_in.at[k, a, i])
            value = value + near_in[k, a, i].astype(F32)
        return value

    def sum_across(k):
        x_out[k] = own_sum(k, 0).astype(BF16)
        red(k, 8, x_out.at[k], x_in.at[k], across)

    def block_of(k, i, far, near, x):
        if i < 2:
            return far.at[k, i]
        return near.at[k, (i - 2) // 2, (i - 2) % 2] if i < 6 else x.at[k]

    def direct_results(k):
        for offset in DIRECT:
            src = block_of(k, offset - 1, far_out, near_out, x_out)
            dst = block_of(k, offset - 1, far_in, near_in, x_in)
            src[...] = result(lax.rem(chip + offset, CHIPS)).astype(BF16)
            red(k, offset - 1, src, dst, mate(offset))

    def back_copy(d):
        return remote(
            back_out.at[d], back_in.at[d], back_send.at[d], back_recv.at[d], peer(nz - steps[d])
        )

    def give_back(k):
        if REDUCE[k] == "D":
            value = part_own[k, 1]
            for i in range(CHIPS - 1):
                ref = block_of(k, i, far_in, near_in, x_in)
                red_wait(k, i, ref)
                value = value + ref[...].astype(F32)
        else:
            value = own_sum(k, 1)
            red_wait(k, 8, x_in.at[k])
            value = value + x_in[k].astype(F32)
        back_out[k * slots_chunk : (k + 1) * slots_chunk] = to_messages(value)
        slots_of(k, lambda d: back_copy(d).start())
        if k == 0:
            @pl.when(core == 0)
            def _():
                back_in[0] = back_out[0]

    begun = []

    def combine(k):
        slots_of(k, lambda d: back_copy(d).wait_recv())
        values = to_rows(back_in[k * slots_chunk : (k + 1) * slots_chunk])
        part = 256.0 * jnp.dot(pick_hi[k], values, preferred_element_type=F32) + jnp.dot(
            pick_lo[k], values, preferred_element_type=F32
        )
        total[...] = total[...] + part if begun else part
        begun.append(k)

    tasks = {
        "A": arrive,
        "X": arrive_across,
        "F1L": lambda k: pass_on(k, 1, True),
        "F1R": lambda k: pass_on(k, 1, False),
        "F0L": lambda k: pass_on(k, 0, True),
        "F0R": lambda k: pass_on(k, 0, False),
        "G": far_across,
        "H": hidden,
        "S0": lambda k: far_results(k, 0),
        "S1": lambda k: far_results(k, 1),
        "SN": near_results,
        "SO": own_results,
        "N0R": lambda k: near_sum(k, 0, 0),
        "N0L": lambda k: near_sum(k, 0, 1),
        "N1R": lambda k: near_sum(k, 1, 0),
        "N1L": lambda k: near_sum(k, 1, 1),
        "O0": sum_across,
        "S": direct_results,
        "O1": give_back,
        "C": combine,
    }
    for name, k in ORDER:
        tasks[name](k)

    answer = total[...] / 65536.0
    comb[0] = answer[:, :LANES]
    comb[1] = answer[:, LANES:]
    comb_copy = remote(comb.at[1 - core], comb_in, one_send.at[3], one_recv.at[3], sibling)
    comb_copy.start()
    for copy in [tok_copy, win_copy, wout_copy] + sends:
        copy.wait_send()
    for k in range(CHUNKS):
        slots_of(k, lambda d: disp_copy(d).wait_send())
        slots_of(k, lambda d: back_copy(d).wait_send())
    comb_copy.wait_recv()
    out[...] = (tok2[core].astype(F32) + gate[...] * (comb[core] + comb_in[...])).astype(BF16)
    comb_copy.wait_send()


DIRECT = (2, 6, 1, 7, 3, 5, 4)


def shards(
    tokens, mod_shift, mod_scale, res_gate, weight_in, weight_out, expert_slot, routes, gate_fixed
):
    n_tok = lax.axis_size("tok")
    nz = n_tok // 2
    count = tokens.shape[0]
    units = weight_in.shape[2]
    rows = nz // CHUNKS * CAP
    hbm = pl.BlockSpec(memory_space=pltpu.HBM)
    dma = pltpu.SemaphoreType.DMA
    scratch = [
        pltpu.VMEM((1, D), F32),
        pltpu.VMEM((1, D), F32),
        pltpu.VMEM((1, LANES), F32),
        pltpu.VMEM((2, count), jnp.int32),
        pltpu.VMEM((2, count), jnp.int32),
        pltpu.VMEM((1, n_tok), jnp.int32),
        pltpu.VMEM((2, count, LANES), BF16),
        pltpu.VMEM((nz, 2 * CAP, LANES), BF16),
        pltpu.VMEM((nz, 2 * CAP, LANES), BF16),
        pltpu.VMEM((CHUNKS, CHIPS, rows, WIDE), BF16),
        pltpu.VMEM((rows, D), BF16),
        pltpu.VMEM((2, D, units), BF16),
        pltpu.VMEM((2, units, D), BF16),
        pltpu.VMEM((2, rows, units), BF16),
        pltpu.VMEM((CHUNKS, 2, rows, WIDE), F32),
        pltpu.VMEM((2, 2, rows, WIDE), F32),
        pltpu.VMEM((CHUNKS, 2, rows, WIDE), BF16),
        pltpu.VMEM((CHUNKS, 2, rows, WIDE), BF16),
        pltpu.VMEM((CHUNKS, 2, 2, rows, WIDE), BF16),
        pltpu.VMEM((CHUNKS, 2, 2, rows, WIDE), BF16),
        pltpu.VMEM((CHUNKS, rows, WIDE), BF16),
        pltpu.VMEM((CHUNKS, rows, WIDE), BF16),
        pltpu.VMEM((nz, 2 * CAP, LANES), BF16),
        pltpu.VMEM((nz, 2 * CAP, LANES), BF16),
        pltpu.VMEM((CHUNKS, count, rows), BF16),
        pltpu.VMEM((CHUNKS, count, rows), BF16),
        pltpu.VMEM((count, WIDE), F32),
        pltpu.VMEM((2, count, LANES), F32),
        pltpu.VMEM((count, LANES), F32),
        dma((9,)),
        dma((4,)),
        dma((4,)),
        dma((nz,)),
        dma((nz,)),
        dma((CHUNKS, 9)),
        dma((CHUNKS, 9)),
        dma((CHUNKS, 9)),
        dma((CHUNKS, 9)),
        dma((nz,)),
        dma((nz,)),
    ]
    return pl.pallas_call(
        functools.partial(kernel, n_tok),
        out_shape=jax.ShapeDtypeStruct(tokens.shape, BF16),
        in_specs=[hbm] * 9,
        out_specs=pl.BlockSpec(memory_space=pltpu.VMEM),
        scratch_shapes=scratch,
        compiler_params=pltpu.CompilerParams(
            collective_id=0, has_side_effects=True, vmem_limit_bytes=60 * 1024 * 1024
        ),
        cost_estimate=pl.CostEstimate(
            flops=4 * 2 * rows * CHUNKS * D * units,
            bytes_accessed=4 * D * units,
            transcendentals=2 * rows * CHUNKS * units,
        ),
    )(
        tokens,
        mod_shift[None, :],
        mod_scale[None, :],
        res_gate[None, :],
        routes.T,
        gate_fixed.T,
        expert_slot[None, :],
        weight_in,
        weight_out,
    )


def solution(mesh):
    placed = (
        P("tok", "place"),
        P(),
        P(),
        P(),
        P("tok", None, "place"),
        P("tok", "place", None),
        P(),
        P("tok", None),
        P("tok", None),
    )
    return jax.shard_map(
        shards, mesh=mesh, in_specs=placed, out_specs=P("tok", "place"), check_vma=False
    )
```

```python
import functools

import jax
import jax.numpy as jnp
from jax import lax
from jax.experimental import pallas as pl
from jax.experimental.pallas import tpu as pltpu
from jax.sharding import PartitionSpec as P

D = 2048
CAP = 24
STEPS = (0, 14, 1, 15, 4, 13, 3, 2, 8, 11, 6, 5, 12, 7, 9, 10)
SIZES = (4, 4, 4, 4)
SENDS = (0, 2, 1, 3)
CHUNKS = len(SIZES)
GATHER = "DBDD"
REDUCE = "ADDD"
ORDER = (
    ("A", 0), ("A", 2), ("A", 1), ("H", 0), ("A", 3), ("S0", 0), ("S1", 0), ("SN", 0), ("SO", 0), ("H", 2),
    ("F1L", 1), ("F1R", 1), ("S", 2), ("SO", 2), ("N0R", 0), ("N0L", 0), ("H", 3), ("G", 1), ("N1R", 0),
    ("N1L", 0), ("S", 3), ("SO", 3), ("O0", 0), ("O1", 2), ("H", 1), ("S", 1), ("SO", 1), ("O1", 3),
    ("O1", 0), ("C", 2), ("O1", 1), ("C", 0), ("C", 3), ("C", 1),
)
CHIPS = 8
PLACES = 16
LANES = 128
WIDE = 256
MESH = pl.DeviceIdType.MESH
F32 = jnp.float32
BF16 = jnp.bfloat16


def remote(src, dst, send_sem, recv_sem, device):
    return pltpu.make_async_remote_copy(
        src_ref=src,
        dst_ref=dst,
        send_sem=send_sem,
        recv_sem=recv_sem,
        device_id=device,
        device_id_type=MESH,
    )


def lane_of(kinds, k, i):
    return sum(1 if kind == "D" else 9 for kind in kinds[:k]) + (0 if kinds[k : k + 1] == "D" else i)


def to_rows(block):
    slots = block.shape[0]
    wide = block.astype(F32)
    halves = [wide[:, h * CAP : (h + 1) * CAP].reshape(slots * CAP, LANES) for h in range(2)]
    return jnp.concatenate(halves, axis=1).astype(BF16)


def to_messages(rows):
    slots = rows.shape[0] // CAP
    halves = [rows[:, h * LANES : (h + 1) * LANES].reshape(slots, CAP, LANES) for h in range(2)]
    return jnp.concatenate(halves, axis=1).astype(BF16)


def kernel(
    n_tok,
    tokens_hbm,
    shift_hbm,
    scale_hbm,
    gate_hbm,
    routes_hbm,
    fixed_hbm,
    catalog_hbm,
    w_in,
    w_out,
    out,
    shift,
    scale,
    gate,
    routes,
    fixed,
    catalog,
    tok2,
    sent_rows,
    got_rows,
    held,
    normed,
    win,
    wout,
    hid,
    part_own,
    part_near,
    far_out,
    far_in,
    near_out,
    near_in,
    x_out,
    x_in,
    all_out,
    all_in,
    back_out,
    back_in,
    pick_hi,
    pick_lo,
    total,
    comb,
    comb_in,
    w_sem,
    one_send,
    one_recv,
    disp_send,
    disp_recv,
    gat_send,
    gat_recv,
    red_send,
    red_recv,
    back_send,
    back_recv,
):
    place, tok = lax.axis_index("place"), lax.axis_index("tok")
    nz = n_tok // 2
    steps = STEPS
    starts = [sum(SIZES[:k]) for k in range(CHUNKS)]
    spans = [slice(start, start + size) for start, size in zip(starts, SIZES)]
    counts = [size * CAP for size in SIZES]
    whole = [pl.ds(0, rows) for rows in counts]
    first = (slice(None), pl.ds(0, LANES))
    second = (slice(None), pl.ds(LANES, LANES))
    home = steps.index(0)
    core, chip = lax.rem(place, 2), lax.div(place, 2)
    xh, y = lax.rem(chip, 2), lax.div(chip, 2)
    z, xl = lax.div(tok, 2), lax.rem(tok, 2)
    sibling = (place + 1 - 2 * core, tok)
    across = (place + 2 - 4 * xh, tok)
    y_right, y_left, y_far = lax.rem(y + 1, 4), lax.rem(y + 3, 4), lax.rem(y + 2, 4)
    right = (y_right * 4 + xh * 2 + core, tok)
    left = (y_left * 4 + xh * 2 + core, tok)

    def chip_at(dy, dx):
        return lax.rem(y + dy, 4) * 2 + lax.rem(xh + dx, 2)

    def chunk_of(d):
        return max(k for k in range(CHUNKS) if starts[k] <= d)

    def per_chunk(k, act):
        if starts[k] == home:
            pl.when(core == 1)(lambda: act(pl.ds(home, SIZES[k])))
            if SIZES[k] > 1:
                pl.when(core == 0)(lambda: act(pl.ds(home + 1, SIZES[k] - 1)))
        else:
            act(pl.ds(starts[k], SIZES[k]))

    def took(sem, ref):
        remote(ref, ref, sem, sem, across).wait_recv()

    def mate(dy, dx):
        return (chip_at(dy, dx) * 2 + core, tok)

    def peer(dz):
        return (place, lax.rem(z + dz, nz) * 2 + lax.rem(xl + core, 2))

    def piece(y_of, a):
        return y_of * 2 + lax.rem(xh + 1 + a, 2)

    barrier = pltpu.get_barrier_semaphore()

    def greet(device):
        pl.semaphore_signal(barrier, inc=1, device_id=device, device_id_type=MESH)

    for dz in sorted(steps, key=lambda dz: -min(dz, nz - dz)):
        if dz:
            greet(peer(dz))

    @pl.when(core == 1)
    def _():
        greet(peer(0))

    for dy, dx in DIRECT:
        greet(mate(dy, dx))
    greet(sibling)

    lanes = pl.ds(pl.multiple_of(chip * WIDE, WIDE), WIDE)
    my_lanes = pl.ds(pl.multiple_of(place * LANES, LANES), LANES)
    pairs = (
        (routes_hbm, routes),
        (catalog_hbm, catalog),
        (tokens_hbm, tok2.at[core]),
        (fixed_hbm, fixed),
        (scale_hbm, scale),
        (shift_hbm, shift),
        (gate_hbm.at[:, my_lanes], gate),
        (w_in.at[0], win.at[core]),
        (w_out.at[0], wout.at[core]),
    )
    loads = [pltpu.make_async_copy(src, dst, w_sem.at[i]) for i, (src, dst) in enumerate(pairs)]
    for copy in loads:
        copy.start()

    loads[0].wait()
    loads[1].wait()
    count = tokens_hbm.shape[0]
    experts = catalog.shape[1]
    kinds = lax.broadcasted_iota(jnp.int32, (experts, count), 0)
    small_eye = lax.broadcasted_iota(jnp.int32, (experts, experts), 0) == lax.broadcasted_iota(
        jnp.int32, (experts, experts), 1
    )
    slot_column = jnp.sum(
        jnp.where(small_eye, catalog[...].astype(F32), 0.0), axis=1, keepdims=True
    )
    ones = [jnp.where(kinds == routes[k : k + 1, :], 1.0, 0.0) for k in range(2)]
    down = lax.broadcasted_iota(jnp.int32, (count, count), 0)
    along = lax.broadcasted_iota(jnp.int32, (count, count), 1)
    earlier = jnp.dot(
        (ones[0] + ones[1]).astype(BF16),
        jnp.where(down < along, 1.0, 0.0).astype(BF16),
        preferred_element_type=F32,
    )
    target = []
    for k in range(2):
        position = jnp.sum(ones[k] * earlier, axis=0, keepdims=True).astype(jnp.int32)
        slot = jnp.sum(ones[k] * slot_column, axis=0, keepdims=True).astype(jnp.int32)
        dz = jnp.bitwise_and((slot >> 1) - z + nz, nz - 1)
        order = jnp.zeros_like(dz)
        for d, step in enumerate(steps):
            order = jnp.where(dz == step, d, order)
        mine = jnp.bitwise_and(slot + xl, 1) == core
        target.append(jnp.where(mine, order * CAP + position, -1))
    every = lax.broadcasted_iota(jnp.int32, (nz * CAP, count), 0)
    pick = jnp.where((every == target[0]) | (every == target[1]), 1.0, 0.0).astype(BF16)

    pl.semaphore_wait(barrier, CHIPS + nz - 1 + core)
    tok_copy = remote(tokens_hbm, tok2.at[core], one_send.at[0], one_recv.at[0], sibling)
    win_copy = remote(w_in.at[0], win.at[core], one_send.at[1], one_recv.at[1], sibling)
    wout_copy = remote(w_out.at[0], wout.at[core], one_send.at[2], one_recv.at[2], sibling)
    tok_copy.start()
    loads[2].wait()
    remote(tokens_hbm, tok2.at[1 - core], one_send.at[0], one_recv.at[0], sibling).wait_recv()

    picked = jnp.dot(
        pick, jnp.concatenate([tok2[0], tok2[1]], axis=1), preferred_element_type=F32
    )
    sent_rows[...] = to_messages(picked)

    def disp_copy(d):
        at = chunk_of(d)
        return remote(
            sent_rows.at[d], got_rows.at[d], disp_send.at[at], disp_recv.at[at], peer(steps[d])
        )

    def slots_of(k, act):
        for d in range(starts[k], starts[k] + SIZES[k]):
            if d == home:
                pl.when(core == 1)(functools.partial(act, d))
            else:
                act(d)

    for k in SENDS:
        slots_of(k, lambda d: disp_copy(d).start())

    @pl.when(core == 0)
    def _():
        got_rows[home] = sent_rows[home]

    win_copy.start()
    wout_copy.start()
    for i in range(3, 7):
        loads[i].wait()

    def as_column(row):
        return jnp.sum(jnp.where(down == along, row, 0.0), axis=1, keepdims=True)

    column = [as_column(t.astype(F32)) for t in target]
    high, low = [], []
    for k in range(2):
        value = fixed[k : k + 1, :]
        high.append(as_column((value >> 8).astype(F32)))
        low.append(as_column(jnp.bitwise_and(value, 255).astype(F32)))
    for k in range(CHUNKS):
        lane = (
            lax.broadcasted_iota(jnp.int32, (count, counts[k]), 1) + starts[k] * CAP
        ).astype(F32)
        for ref, part in ((pick_hi, high), (pick_lo, low)):
            ref[k, :, : counts[k]] = (
                jnp.where(lane == column[0], part[0], 0.0)
                + jnp.where(lane == column[1], part[1], 0.0)
            ).astype(BF16)

    def gat(k, i, ref, to):
        remote(ref, ref, gat_send.at[k], gat_recv.at[lane_of(GATHER, k, i)], to).start()

    def gat_wait(k, i, ref):
        took(gat_recv.at[lane_of(GATHER, k, i)], ref)

    def red(k, i, src, dst, to):
        remote(src, dst, red_send.at[k], red_recv.at[lane_of(REDUCE, k, i)], to).start()

    def red_wait(k, i, ref):
        took(red_recv.at[lane_of(REDUCE, k, i)], ref)

    def piece_ref(k, q):
        return held.at[k, q, whole[k]]

    def arrive(k):
        per_chunk(k, lambda slots: took(disp_recv.at[k], got_rows.at[slots]))
        held[k, chip, whole[k]] = to_rows(got_rows[spans[k]])
        mine = piece_ref(k, chip)
        if GATHER[k] == "D":
            for i, (dy, dx) in enumerate(DIRECT):
                gat(k, i, mine, mate(dy, dx))
        else:
            gat(k, 0, mine, across)
            gat(k, 1, mine, right)
            gat(k, 2, mine, left)

    def arrive_across(k):
        other = piece_ref(k, piece(y, 0))
        gat_wait(k, 0, other)
        gat(k, 3, other, right)
        gat(k, 4, other, left)

    def pass_on(k, a, from_left):
        i = 1 + 2 * (1 - a) + (0 if from_left else 1)
        ref = piece_ref(k, piece(y_left if from_left else y_right, a))
        gat_wait(k, i, ref)
        gat(k, i + 4, ref.at[first if from_left else second], right if from_left else left)
        if GATHER[k] == "B":
            gat(k, i + 2, ref, across)

    def far_across(k):
        far = piece_ref(k, piece(y_far, 1))
        gat_wait(k, 5, far.at[first])
        gat_wait(k, 6, far.at[second])
        gat(k, 7, far, across)

    def all_there(k):
        if GATHER[k] == "D":
            gat_wait(k, 0, held.at[k, pl.ds(0, CHIPS - 1), whole[k]])
        elif GATHER[k] == "B":
            gat_wait(k, 0, piece_ref(k, piece(y, 0)))
            gat_wait(k, 3, piece_ref(k, piece(y_left, 0)))
            gat_wait(k, 4, piece_ref(k, piece(y_right, 0)))
            gat_wait(k, 7, piece_ref(k, piece(y_far, 0)))
        else:
            for a in range(2):
                far = piece_ref(k, piece(y_far, a))
                gat_wait(k, 7 - 2 * a, far.at[first])
                gat_wait(k, 8 - 2 * a, far.at[second])

    tiles = win.shape[2] // WIDE
    ready = []

    def hidden(k):
        all_there(k)
        rows = whole[k]
        sums = jnp.zeros((counts[k], WIDE), F32)
        squares = jnp.zeros((counts[k], WIDE), F32)
        for q in range(CHIPS):
            x = held[k, q, rows].astype(F32)
            sums += x
            squares += x * x
        mean = jnp.sum(sums, axis=1, keepdims=True) / D
        inverse = lax.rsqrt(jnp.sum(squares, axis=1, keepdims=True) / D - mean * mean + 1e-06)
        for q in range(CHIPS):
            at = slice(q * WIDE, (q + 1) * WIDE)
            x = held[k, q, rows].astype(F32)
            normed[rows, at] = (
                (x - mean) * inverse * (1.0 + scale[:, at]) + shift[:, at]
            ).astype(BF16)
        if not ready:
            ready.append(k)
            loads[7].wait()
            loads[8].wait()
            for i, (src, dst) in ((1, (w_in, win)), (2, (w_out, wout))):
                remote(src.at[0], dst.at[1 - core], one_send.at[i], one_recv.at[i], sibling).wait_recv()
        for c in range(2):
            for t in range(tiles):
                at = slice(t * WIDE, (t + 1) * WIDE)
                h = jnp.dot(normed[rows, :], win[c, :, at], preferred_element_type=F32)
                hid[c, rows, at] = jax.nn.gelu(h, approximate=True).astype(BF16)

    def result(k, q):
        at = pl.ds(pl.multiple_of(q * WIDE, WIDE), WIDE)
        return jnp.dot(hid[0, whole[k]], wout[0, :, at], preferred_element_type=F32) + jnp.dot(
            hid[1, whole[k]], wout[1, :, at], preferred_element_type=F32
        )

    def far_results(k, a):
        far_out[k, a, whole[k]] = result(k, piece(y_far, a)).astype(BF16)
        for i, (part, to) in enumerate(((first, right), (second, left))):
            src, dst = far_out.at[k, a, whole[k]].at[part], far_in.at[k, a, whole[k]].at[part]
            red(k, 2 * i + a, src, dst, to)

    def near_results(k):
        for a in range(2):
            part_near[a, 0, whole[k]] = result(k, piece(y_right, a))
            part_near[a, 1, whole[k]] = result(k, piece(y_left, a))

    def own_results(k):
        if REDUCE[k] == "D":
            part_own[k, 1, whole[k]] = result(k, chip)
        else:
            for a in range(2):
                part_own[k, a, whole[k]] = result(k, piece(y, a))

    def near_sum(k, a, i):
        here, rest = (0, LANES) if i == 0 else (LANES, 0)
        got = far_in.at[k, a, whole[k]]
        red_wait(k, 2 * i + a, got.at[first if i == 0 else second])
        for at, add in ((pl.ds(here, LANES), True), (pl.ds(rest, LANES), False)):
            value = part_near[a, i, whole[k], at]
            if add:
                value = value + far_in[k, a, whole[k], at].astype(F32)
            near_out[k, a, i, whole[k], at] = value.astype(BF16)
        j = 4 + 2 * i + a
        src, dst = near_out.at[k, a, i, whole[k]], near_in.at[k, a, i, whole[k]]
        red(k, j, src, dst, right if i == 0 else left)

    def own_sum(k, a):
        value = part_own[k, a, whole[k]]
        for i in range(2):
            red_wait(k, 4 + 2 * i + a, near_in.at[k, a, i, whole[k]])
            value = value + near_in[k, a, i, whole[k]].astype(F32)
        return value

    def sum_across(k):
        x_out[k, whole[k]] = own_sum(k, 0).astype(BF16)
        red(k, 8, x_out.at[k, whole[k]], x_in.at[k, whole[k]], across)

    def direct_results(k):
        for i, (dy, dx) in enumerate(DIRECT):
            src, dst = all_out.at[k, i, whole[k]], all_in.at[k, i, whole[k]]
            src[...] = result(k, chip_at(dy, dx)).astype(BF16)
            red(k, i, src, dst, mate(dy, dx))

    def back_copy(d):
        at = chunk_of(d)
        return remote(
            back_out.at[d], back_in.at[d], back_send.at[at], back_recv.at[at], peer(nz - steps[d])
        )

    def give_back(k):
        if REDUCE[k] == "D":
            value = part_own[k, 1, whole[k]]
            red_wait(k, 0, all_in.at[k, :, whole[k]])
            for i in range(CHIPS - 1):
                value = value + all_in[k, i, whole[k]].astype(F32)
        else:
            value = own_sum(k, 1)
            red_wait(k, 8, x_in.at[k, whole[k]])
            value = value + x_in[k, whole[k]].astype(F32)
        back_out[spans[k]] = to_messages(value)
        slots_of(k, lambda d: back_copy(d).start())
        if starts[k] <= home < starts[k] + SIZES[k]:
            @pl.when(core == 0)
            def _():
                back_in[home] = back_out[home]

    begun = []

    def combine(k):
        per_chunk(k, lambda slots: took(back_recv.at[k], back_in.at[slots]))
        values = to_rows(back_in[spans[k]])
        at = slice(0, counts[k])
        part = 256.0 * jnp.dot(pick_hi[k, :, at], values, preferred_element_type=F32) + jnp.dot(
            pick_lo[k, :, at], values, preferred_element_type=F32
        )
        total[...] = total[...] + part if begun else part
        begun.append(k)

    tasks = {
        "A": arrive,
        "X": arrive_across,
        "F1L": lambda k: pass_on(k, 1, True),
        "F1R": lambda k: pass_on(k, 1, False),
        "F0L": lambda k: pass_on(k, 0, True),
        "F0R": lambda k: pass_on(k, 0, False),
        "G": far_across,
        "H": hidden,
        "S0": lambda k: far_results(k, 0),
        "S1": lambda k: far_results(k, 1),
        "SN": near_results,
        "SO": own_results,
        "N0R": lambda k: near_sum(k, 0, 0),
        "N0L": lambda k: near_sum(k, 0, 1),
        "N1R": lambda k: near_sum(k, 1, 0),
        "N1L": lambda k: near_sum(k, 1, 1),
        "O0": sum_across,
        "S": direct_results,
        "O1": give_back,
        "C": combine,
    }
    for name, k in ORDER:
        tasks[name](k)

    answer = total[...] / 65536.0
    comb[0] = answer[:, :LANES]
    comb[1] = answer[:, LANES:]
    comb_copy = remote(comb.at[1 - core], comb_in, one_send.at[3], one_recv.at[3], sibling)
    comb_copy.start()
    for copy in (tok_copy, win_copy, wout_copy):
        copy.wait_send()
    for k in range(CHUNKS):
        took(gat_send.at[k], held.at[k, pl.ds(0, CHIPS - 1), whole[k]])
        took(red_send.at[k], all_out.at[k, :, whole[k]])
        per_chunk(k, lambda slots: took(disp_send.at[k], sent_rows.at[slots]))
        per_chunk(k, lambda slots: took(back_send.at[k], back_out.at[slots]))
    comb_copy.wait_recv()
    out[...] = (tok2[core].astype(F32) + gate[...] * (comb[core] + comb_in[...])).astype(BF16)
    comb_copy.wait_send()


DIRECT = ((2, 1), (1, 1), (3, 1), (2, 0), (0, 1), (1, 0), (3, 0))


def shards(
    tokens, mod_shift, mod_scale, res_gate, weight_in, weight_out, expert_slot, routes, gate_fixed
):
    n_tok = lax.axis_size("tok")
    nz = n_tok // 2
    count = tokens.shape[0]
    units = weight_in.shape[2]
    rows = max(SIZES) * CAP
    hbm = pl.BlockSpec(memory_space=pltpu.HBM)
    dma = pltpu.SemaphoreType.DMA
    scratch = [
        pltpu.VMEM((1, D), F32),
        pltpu.VMEM((1, D), F32),
        pltpu.VMEM((1, LANES), F32),
        pltpu.VMEM((2, count), jnp.int32),
        pltpu.VMEM((2, count), jnp.int32),
        pltpu.VMEM((1, n_tok), jnp.int32),
        pltpu.VMEM((2, count, LANES), BF16),
        pltpu.VMEM((nz, 2 * CAP, LANES), BF16),
        pltpu.VMEM((nz, 2 * CAP, LANES), BF16),
        pltpu.VMEM((CHUNKS, CHIPS, rows, WIDE), BF16),
        pltpu.VMEM((rows, D), BF16),
        pltpu.VMEM((2, D, units), BF16),
        pltpu.VMEM((2, units, D), BF16),
        pltpu.VMEM((2, rows, units), BF16),
        pltpu.VMEM((CHUNKS, 2, rows, WIDE), F32),
        pltpu.VMEM((2, 2, rows, WIDE), F32),
        pltpu.VMEM((CHUNKS, 2, rows, WIDE), BF16),
        pltpu.VMEM((CHUNKS, 2, rows, WIDE), BF16),
        pltpu.VMEM((CHUNKS, 2, 2, rows, WIDE), BF16),
        pltpu.VMEM((CHUNKS, 2, 2, rows, WIDE), BF16),
        pltpu.VMEM((CHUNKS, rows, WIDE), BF16),
        pltpu.VMEM((CHUNKS, rows, WIDE), BF16),
        pltpu.VMEM((CHUNKS, CHIPS - 1, rows, WIDE), BF16),
        pltpu.VMEM((CHUNKS, CHIPS - 1, rows, WIDE), BF16),
        pltpu.VMEM((nz, 2 * CAP, LANES), BF16),
        pltpu.VMEM((nz, 2 * CAP, LANES), BF16),
        pltpu.VMEM((CHUNKS, count, rows), BF16),
        pltpu.VMEM((CHUNKS, count, rows), BF16),
        pltpu.VMEM((count, WIDE), F32),
        pltpu.VMEM((2, count, LANES), F32),
        pltpu.VMEM((count, LANES), F32),
        dma((9,)),
        dma((4,)),
        dma((4,)),
        dma((CHUNKS,)),
        dma((CHUNKS,)),
        dma((CHUNKS,)),
        dma((lane_of(GATHER, CHUNKS, 0),)),
        dma((CHUNKS,)),
        dma((lane_of(REDUCE, CHUNKS, 0),)),
        dma((CHUNKS,)),
        dma((CHUNKS,)),
    ]
    return pl.pallas_call(
        functools.partial(kernel, n_tok),
        out_shape=jax.ShapeDtypeStruct(tokens.shape, BF16),
        in_specs=[hbm] * 9,
        out_specs=pl.BlockSpec(memory_space=pltpu.VMEM),
        scratch_shapes=scratch,
        compiler_params=pltpu.CompilerParams(
            collective_id=0, has_side_effects=True, vmem_limit_bytes=60 * 1024 * 1024
        ),
        cost_estimate=pl.CostEstimate(
            flops=4 * 2 * nz * CAP * D * units,
            bytes_accessed=4 * D * units,
            transcendentals=2 * nz * CAP * units,
        ),
    )(
        tokens,
        mod_shift[None, :],
        mod_scale[None, :],
        res_gate[None, :],
        routes.T,
        gate_fixed.T,
        expert_slot[None, :],
        weight_in,
        weight_out,
    )


def solution(mesh):
    placed = (
        P("tok", "place"),
        P(),
        P(),
        P(),
        P("tok", None, "place"),
        P("tok", "place", None),
        P(),
        P("tok", None),
        P("tok", None),
    )
    return jax.shard_map(
        shards, mesh=mesh, in_specs=placed, out_specs=P("tok", "place"), check_vma=False
    )
```

```python
import functools

import jax
import jax.numpy as jnp
from jax import lax
from jax.experimental import pallas as pl
from jax.experimental.pallas import tpu as pltpu
from jax.sharding import PartitionSpec as P

D = 2048
CAP = 24
STEPS = (0, 14, 1, 15, 4, 13, 3, 2, 8, 11, 6, 5, 12, 7, 9, 10)
SIZES = (4, 4, 4, 4)
SENDS = (0, 2, 1, 3)
CHUNKS = len(SIZES)
GATHER = "DBDD"
REDUCE = "ADDD"
ORDER = (
    ("A", 0), ("A", 2), ("A", 1), ("H", 0), ("A", 3), ("S0", 0), ("S1", 0), ("SN", 0), ("SO", 0), ("H", 2),
    ("F1L", 1), ("F1R", 1), ("S", 2), ("SO", 2), ("N0R", 0), ("N0L", 0), ("H", 3), ("G", 1), ("N1R", 0),
    ("N1L", 0), ("S", 3), ("SO", 3), ("O0", 0), ("O1", 2), ("H", 1), ("S", 1), ("SO", 1), ("O1", 3),
    ("O1", 0), ("C", 2), ("O1", 1), ("C", 0), ("C", 3), ("C", 1),
)
CHIPS = 8
PLACES = 16
LANES = 128
WIDE = 256
MESH = pl.DeviceIdType.MESH
F32 = jnp.float32
BF16 = jnp.bfloat16


def remote(src, dst, send_sem, recv_sem, device):
    return pltpu.make_async_remote_copy(
        src_ref=src,
        dst_ref=dst,
        send_sem=send_sem,
        recv_sem=recv_sem,
        device_id=device,
        device_id_type=MESH,
    )


SHARED = {"D": (0,) * 7, "B": (0, 1, 2, 0, 0, 3, 3, 0), "A": (0, 1, 2, 3, 4, 5, 4, 5, 5)}


def lane_of(kinds, k, i):
    before = sum(max(SHARED[kind]) + 1 for kind in kinds[:k])
    return before + (SHARED[kinds[k]][i] if k < len(kinds) else 0)


def to_rows(block):
    slots = block.shape[0]
    wide = block.astype(F32)
    halves = [wide[:, h * CAP : (h + 1) * CAP].reshape(slots * CAP, LANES) for h in range(2)]
    return jnp.concatenate(halves, axis=1).astype(BF16)


def to_messages(rows):
    slots = rows.shape[0] // CAP
    halves = [rows[:, h * LANES : (h + 1) * LANES].reshape(slots, CAP, LANES) for h in range(2)]
    return jnp.concatenate(halves, axis=1).astype(BF16)


def kernel(
    n_tok,
    tokens_hbm,
    shift_hbm,
    scale_hbm,
    gate_hbm,
    routes_hbm,
    fixed_hbm,
    catalog_hbm,
    w_in,
    w_out,
    out,
    shift,
    scale,
    gate,
    routes,
    fixed,
    catalog,
    tok2,
    sent_rows,
    got_rows,
    held,
    normed,
    win,
    wout,
    hid,
    part_own,
    part_near,
    far_out,
    far_in,
    near_out,
    near_in,
    x_out,
    x_in,
    all_out,
    all_in,
    back_out,
    back_in,
    pick_hi,
    pick_lo,
    total,
    comb,
    comb_in,
    w_sem,
    one_send,
    one_recv,
    disp_send,
    disp_recv,
    gat_send,
    gat_recv,
    red_send,
    red_recv,
    back_send,
    back_recv,
):
    place, tok = lax.axis_index("place"), lax.axis_index("tok")
    nz = n_tok // 2
    steps = STEPS
    starts = [sum(SIZES[:k]) for k in range(CHUNKS)]
    spans = [slice(start, start + size) for start, size in zip(starts, SIZES)]
    counts = [size * CAP for size in SIZES]
    whole = [pl.ds(0, rows) for rows in counts]
    first = (slice(None), pl.ds(0, LANES))
    second = (slice(None), pl.ds(LANES, LANES))
    home = steps.index(0)
    core, chip = lax.rem(place, 2), lax.div(place, 2)
    xh, y = lax.rem(chip, 2), lax.div(chip, 2)
    z, xl = lax.div(tok, 2), lax.rem(tok, 2)
    sibling = (place + 1 - 2 * core, tok)
    across = (place + 2 - 4 * xh, tok)
    y_right, y_left, y_far = lax.rem(y + 1, 4), lax.rem(y + 3, 4), lax.rem(y + 2, 4)
    right = (y_right * 4 + xh * 2 + core, tok)
    left = (y_left * 4 + xh * 2 + core, tok)

    def chip_at(dy, dx):
        return lax.rem(y + dy, 4) * 2 + lax.rem(xh + dx, 2)

    def chunk_of(d):
        return max(k for k in range(CHUNKS) if starts[k] <= d)

    def per_chunk(k, act):
        if starts[k] == home:
            pl.when(core == 1)(lambda: act(pl.ds(home, SIZES[k])))
            if SIZES[k] > 1:
                pl.when(core == 0)(lambda: act(pl.ds(home + 1, SIZES[k] - 1)))
        else:
            act(pl.ds(starts[k], SIZES[k]))

    def took(sem, ref):
        remote(ref, ref, sem, sem, across).wait_recv()

    def mate(dy, dx):
        return (chip_at(dy, dx) * 2 + core, tok)

    def peer(dz):
        return (place, lax.rem(z + dz, nz) * 2 + lax.rem(xl + core, 2))

    def piece(y_of, a):
        return y_of * 2 + lax.rem(xh + 1 + a, 2)

    barrier = pltpu.get_barrier_semaphore()

    def greet(device):
        pl.semaphore_signal(barrier, inc=1, device_id=device, device_id_type=MESH)

    for dz in sorted(steps, key=lambda dz: -min(dz, nz - dz)):
        if dz:
            greet(peer(dz))

    @pl.when(core == 1)
    def _():
        greet(peer(0))

    for dy, dx in DIRECT:
        greet(mate(dy, dx))
    greet(sibling)

    lanes = pl.ds(pl.multiple_of(chip * WIDE, WIDE), WIDE)
    my_lanes = pl.ds(pl.multiple_of(place * LANES, LANES), LANES)
    pairs = (
        (routes_hbm, routes),
        (catalog_hbm, catalog),
        (tokens_hbm, tok2.at[core]),
        (fixed_hbm, fixed),
        (scale_hbm, scale),
        (shift_hbm, shift),
        (gate_hbm.at[:, my_lanes], gate),
        (w_in.at[0], win.at[core]),
        (w_out.at[0], wout.at[core]),
    )
    loads = [pltpu.make_async_copy(src, dst, w_sem.at[i]) for i, (src, dst) in enumerate(pairs)]
    for copy in loads:
        copy.start()

    loads[0].wait()
    loads[1].wait()
    count = tokens_hbm.shape[0]
    experts = catalog.shape[1]
    kinds = lax.broadcasted_iota(jnp.int32, (experts, count), 0)
    small_eye = lax.broadcasted_iota(jnp.int32, (experts, experts), 0) == lax.broadcasted_iota(
        jnp.int32, (experts, experts), 1
    )
    slot_column = jnp.sum(
        jnp.where(small_eye, catalog[...].astype(F32), 0.0), axis=1, keepdims=True
    )
    ones = [jnp.where(kinds == routes[k : k + 1, :], 1.0, 0.0) for k in range(2)]
    down = lax.broadcasted_iota(jnp.int32, (count, count), 0)
    along = lax.broadcasted_iota(jnp.int32, (count, count), 1)
    earlier = jnp.dot(
        (ones[0] + ones[1]).astype(BF16),
        jnp.where(down < along, 1.0, 0.0).astype(BF16),
        preferred_element_type=F32,
    )
    target = []
    for k in range(2):
        position = jnp.sum(ones[k] * earlier, axis=0, keepdims=True).astype(jnp.int32)
        slot = jnp.sum(ones[k] * slot_column, axis=0, keepdims=True).astype(jnp.int32)
        dz = jnp.bitwise_and((slot >> 1) - z + nz, nz - 1)
        order = jnp.zeros_like(dz)
        for d, step in enumerate(steps):
            order = jnp.where(dz == step, d, order)
        mine = jnp.bitwise_and(slot + xl, 1) == core
        target.append(jnp.where(mine, order * CAP + position, -1))
    every = lax.broadcasted_iota(jnp.int32, (nz * CAP, count), 0)
    pick = jnp.where((every == target[0]) | (every == target[1]), 1.0, 0.0).astype(BF16)

    pl.semaphore_wait(barrier, CHIPS + nz - 1 + core)
    tok_copy = remote(tokens_hbm, tok2.at[core], one_send.at[0], one_recv.at[0], sibling)
    win_copy = remote(w_in.at[0], win.at[core], one_send.at[1], one_recv.at[1], sibling)
    wout_copy = remote(w_out.at[0], wout.at[core], one_send.at[2], one_recv.at[2], sibling)
    tok_copy.start()
    loads[2].wait()
    remote(tokens_hbm, tok2.at[1 - core], one_send.at[0], one_recv.at[0], sibling).wait_recv()

    picked = jnp.dot(
        pick, jnp.concatenate([tok2[0], tok2[1]], axis=1), preferred_element_type=F32
    )
    sent_rows[...] = to_messages(picked)

    def disp_copy(d):
        at = chunk_of(d)
        return remote(
            sent_rows.at[d], got_rows.at[d], disp_send.at[0], disp_recv.at[at], peer(steps[d])
        )

    def slots_of(k, act):
        for d in range(starts[k], starts[k] + SIZES[k]):
            if d == home:
                pl.when(core == 1)(functools.partial(act, d))
            else:
                act(d)

    for k in SENDS:
        slots_of(k, lambda d: disp_copy(d).start())

    @pl.when(core == 0)
    def _():
        got_rows[home] = sent_rows[home]

    win_copy.start()
    wout_copy.start()
    for i in range(3, 7):
        loads[i].wait()

    def as_column(row):
        return jnp.sum(jnp.where(down == along, row, 0.0), axis=1, keepdims=True)

    column = [as_column(t.astype(F32)) for t in target]
    high, low = [], []
    for k in range(2):
        value = fixed[k : k + 1, :]
        high.append(as_column((value >> 8).astype(F32)))
        low.append(as_column(jnp.bitwise_and(value, 255).astype(F32)))
    for k in range(CHUNKS):
        lane = (
            lax.broadcasted_iota(jnp.int32, (count, counts[k]), 1) + starts[k] * CAP
        ).astype(F32)
        for ref, part in ((pick_hi, high), (pick_lo, low)):
            ref[k, :, : counts[k]] = (
                jnp.where(lane == column[0], part[0], 0.0)
                + jnp.where(lane == column[1], part[1], 0.0)
            ).astype(BF16)

    def gat(k, i, ref, to):
        remote(ref, ref, gat_send.at[0], gat_recv.at[lane_of(GATHER, k, i)], to).start()

    def gat_wait(k, i, ref):
        took(gat_recv.at[lane_of(GATHER, k, i)], ref)

    def red(k, i, src, dst, to):
        remote(src, dst, red_send.at[0], red_recv.at[lane_of(REDUCE, k, i)], to).start()

    def red_wait(k, i, ref):
        took(red_recv.at[lane_of(REDUCE, k, i)], ref)

    def piece_ref(k, q):
        return held.at[k, q, whole[k]]

    def arrive(k):
        per_chunk(k, lambda slots: took(disp_recv.at[k], got_rows.at[slots]))
        held[k, chip, whole[k]] = to_rows(got_rows[spans[k]])
        mine = piece_ref(k, chip)
        if GATHER[k] == "D":
            for i, (dy, dx) in enumerate(DIRECT):
                gat(k, i, mine, mate(dy, dx))
        else:
            gat(k, 0, mine, across)
            gat(k, 1, mine, right)
            gat(k, 2, mine, left)

    def arrive_across(k):
        other = piece_ref(k, piece(y, 0))
        gat_wait(k, 0, other)
        gat(k, 3, other, right)
        gat(k, 4, other, left)

    def pass_on(k, a, from_left):
        i = 1 + 2 * (1 - a) + (0 if from_left else 1)
        ref = piece_ref(k, piece(y_left if from_left else y_right, a))
        gat_wait(k, i, ref)
        gat(k, i + 4, ref.at[first if from_left else second], right if from_left else left)
        if GATHER[k] == "B":
            gat(k, i + 2, ref, across)

    def far_across(k):
        far = piece_ref(k, piece(y_far, 1))
        gat_wait(k, 5, far)
        gat(k, 7, far, across)

    def all_there(k):
        if GATHER[k] == "D":
            gat_wait(k, 0, held.at[k, pl.ds(0, CHIPS - 1), whole[k]])
        elif GATHER[k] == "B":
            gat_wait(k, 0, held.at[k, pl.ds(0, 4), whole[k]])
        else:
            for a in range(2):
                far = piece_ref(k, piece(y_far, a))
                gat_wait(k, 7 - 2 * a, far.at[first])
                gat_wait(k, 8 - 2 * a, far.at[second])

    tiles = win.shape[2] // WIDE
    ready = []

    def hidden(k):
        all_there(k)
        rows = whole[k]
        sums = jnp.zeros((counts[k], WIDE), F32)
        squares = jnp.zeros((counts[k], WIDE), F32)
        for q in range(CHIPS):
            x = held[k, q, rows].astype(F32)
            sums += x
            squares += x * x
        mean = jnp.sum(sums, axis=1, keepdims=True) / D
        inverse = lax.rsqrt(jnp.sum(squares, axis=1, keepdims=True) / D - mean * mean + 1e-06)
        for q in range(CHIPS):
            at = slice(q * WIDE, (q + 1) * WIDE)
            x = held[k, q, rows].astype(F32)
            normed[rows, at] = (
                (x - mean) * inverse * (1.0 + scale[:, at]) + shift[:, at]
            ).astype(BF16)
        if not ready:
            ready.append(k)
            loads[7].wait()
            loads[8].wait()
            for i, (src, dst) in ((1, (w_in, win)), (2, (w_out, wout))):
                remote(src.at[0], dst.at[1 - core], one_send.at[i], one_recv.at[i], sibling).wait_recv()
        for c in range(2):
            for t in range(tiles):
                at = slice(t * WIDE, (t + 1) * WIDE)
                h = jnp.dot(normed[rows, :], win[c, :, at], preferred_element_type=F32)
                hid[c, rows, at] = jax.nn.gelu(h, approximate=True).astype(BF16)

    def result(k, q):
        at = pl.ds(pl.multiple_of(q * WIDE, WIDE), WIDE)
        return jnp.dot(hid[0, whole[k]], wout[0, :, at], preferred_element_type=F32) + jnp.dot(
            hid[1, whole[k]], wout[1, :, at], preferred_element_type=F32
        )

    def far_results(k, a):
        far_out[k, a, whole[k]] = result(k, piece(y_far, a)).astype(BF16)
        for i, (part, to) in enumerate(((first, right), (second, left))):
            src, dst = far_out.at[k, a, whole[k]].at[part], far_in.at[k, a, whole[k]].at[part]
            red(k, 2 * i + a, src, dst, to)

    def near_results(k):
        for a in range(2):
            part_near[a, 0, whole[k]] = result(k, piece(y_right, a))
            part_near[a, 1, whole[k]] = result(k, piece(y_left, a))

    def own_results(k):
        if REDUCE[k] == "D":
            part_own[k, 1, whole[k]] = result(k, chip)
        else:
            for a in range(2):
                part_own[k, a, whole[k]] = result(k, piece(y, a))

    def near_sum(k, a, i):
        here, rest = (0, LANES) if i == 0 else (LANES, 0)
        got = far_in.at[k, a, whole[k]]
        red_wait(k, 2 * i + a, got.at[first if i == 0 else second])
        for at, add in ((pl.ds(here, LANES), True), (pl.ds(rest, LANES), False)):
            value = part_near[a, i, whole[k], at]
            if add:
                value = value + far_in[k, a, whole[k], at].astype(F32)
            near_out[k, a, i, whole[k], at] = value.astype(BF16)
        j = 4 + 2 * i + a
        src, dst = near_out.at[k, a, i, whole[k]], near_in.at[k, a, i, whole[k]]
        red(k, j, src, dst, right if i == 0 else left)

    def own_sum(k, a):
        value = part_own[k, a, whole[k]]
        red_wait(k, 4 + a, all_in.at[k, pl.ds(0, 2 + a), whole[k]])
        for i in range(2):
            value = value + near_in[k, a, i, whole[k]].astype(F32)
        return value

    def sum_across(k):
        x_out[k, whole[k]] = own_sum(k, 0).astype(BF16)
        red(k, 8, x_out.at[k, whole[k]], x_in.at[k, whole[k]], across)

    def direct_results(k):
        for i, (dy, dx) in enumerate(DIRECT):
            src, dst = all_out.at[k, i, whole[k]], all_in.at[k, i, whole[k]]
            src[...] = result(k, chip_at(dy, dx)).astype(BF16)
            red(k, i, src, dst, mate(dy, dx))

    def back_copy(d):
        at = chunk_of(d)
        return remote(
            back_out.at[d], back_in.at[d], back_send.at[0], back_recv.at[at], peer(nz - steps[d])
        )

    def give_back(k):
        if REDUCE[k] == "D":
            value = part_own[k, 1, whole[k]]
            red_wait(k, 0, all_in.at[k, :, whole[k]])
            for i in range(CHIPS - 1):
                value = value + all_in[k, i, whole[k]].astype(F32)
        else:
            value = own_sum(k, 1)
            value = value + x_in[k, whole[k]].astype(F32)
        back_out[spans[k]] = to_messages(value)
        slots_of(k, lambda d: back_copy(d).start())
        if starts[k] <= home < starts[k] + SIZES[k]:
            @pl.when(core == 0)
            def _():
                back_in[home] = back_out[home]

    begun = []

    def combine(k):
        per_chunk(k, lambda slots: took(back_recv.at[k], back_in.at[slots]))
        values = to_rows(back_in[spans[k]])
        at = slice(0, counts[k])
        part = 256.0 * jnp.dot(pick_hi[k, :, at], values, preferred_element_type=F32) + jnp.dot(
            pick_lo[k, :, at], values, preferred_element_type=F32
        )
        total[...] = total[...] + part if begun else part
        begun.append(k)

    tasks = {
        "A": arrive,
        "X": arrive_across,
        "F1L": lambda k: pass_on(k, 1, True),
        "F1R": lambda k: pass_on(k, 1, False),
        "F0L": lambda k: pass_on(k, 0, True),
        "F0R": lambda k: pass_on(k, 0, False),
        "G": far_across,
        "H": hidden,
        "S0": lambda k: far_results(k, 0),
        "S1": lambda k: far_results(k, 1),
        "SN": near_results,
        "SO": own_results,
        "N0R": lambda k: near_sum(k, 0, 0),
        "N0L": lambda k: near_sum(k, 0, 1),
        "N1R": lambda k: near_sum(k, 1, 0),
        "N1L": lambda k: near_sum(k, 1, 1),
        "O0": sum_across,
        "S": direct_results,
        "O1": give_back,
        "C": combine,
    }
    for name, k in ORDER:
        tasks[name](k)

    answer = total[...] / 65536.0
    comb[0] = answer[:, :LANES]
    comb[1] = answer[:, LANES:]
    comb_copy = remote(comb.at[1 - core], comb_in, one_send.at[3], one_recv.at[3], sibling)
    comb_copy.start()
    for copy in (tok_copy, win_copy, wout_copy):
        copy.wait_send()
    took(gat_send.at[0], all_out)
    took(red_send.at[0], all_out)

    def sent(slots):
        took(disp_send.at[0], sent_rows.at[slots])
        took(back_send.at[0], back_out.at[slots])

    pl.when(core == 1)(lambda: sent(pl.ds(0, nz)))
    pl.when(core == 0)(lambda: sent(pl.ds(1, nz - 1)))
    comb_copy.wait_recv()
    out[...] = (tok2[core].astype(F32) + gate[...] * (comb[core] + comb_in[...])).astype(BF16)
    comb_copy.wait_send()


DIRECT = ((2, 1), (1, 1), (3, 1), (2, 0), (0, 1), (1, 0), (3, 0))


def shards(
    tokens, mod_shift, mod_scale, res_gate, weight_in, weight_out, expert_slot, routes, gate_fixed
):
    n_tok = lax.axis_size("tok")
    nz = n_tok // 2
    count = tokens.shape[0]
    units = weight_in.shape[2]
    rows = max(SIZES) * CAP
    hbm = pl.BlockSpec(memory_space=pltpu.HBM)
    dma = pltpu.SemaphoreType.DMA
    scratch = [
        pltpu.VMEM((1, D), F32),
        pltpu.VMEM((1, D), F32),
        pltpu.VMEM((1, LANES), F32),
        pltpu.VMEM((2, count), jnp.int32),
        pltpu.VMEM((2, count), jnp.int32),
        pltpu.VMEM((1, n_tok), jnp.int32),
        pltpu.VMEM((2, count, LANES), BF16),
        pltpu.VMEM((nz, 2 * CAP, LANES), BF16),
        pltpu.VMEM((nz, 2 * CAP, LANES), BF16),
        pltpu.VMEM((CHUNKS, CHIPS, rows, WIDE), BF16),
        pltpu.VMEM((rows, D), BF16),
        pltpu.VMEM((2, D, units), BF16),
        pltpu.VMEM((2, units, D), BF16),
        pltpu.VMEM((2, rows, units), BF16),
        pltpu.VMEM((CHUNKS, 2, rows, WIDE), F32),
        pltpu.VMEM((2, 2, rows, WIDE), F32),
        pltpu.VMEM((CHUNKS, 2, rows, WIDE), BF16),
        pltpu.VMEM((CHUNKS, 2, rows, WIDE), BF16),
        pltpu.VMEM((CHUNKS, 2, 2, rows, WIDE), BF16),
        pltpu.VMEM((CHUNKS, 2, 2, rows, WIDE), BF16),
        pltpu.VMEM((CHUNKS, rows, WIDE), BF16),
        pltpu.VMEM((CHUNKS, rows, WIDE), BF16),
        pltpu.VMEM((CHUNKS, CHIPS - 1, rows, WIDE), BF16),
        pltpu.VMEM((CHUNKS, CHIPS - 1, rows, WIDE), BF16),
        pltpu.VMEM((nz, 2 * CAP, LANES), BF16),
        pltpu.VMEM((nz, 2 * CAP, LANES), BF16),
        pltpu.VMEM((CHUNKS, count, rows), BF16),
        pltpu.VMEM((CHUNKS, count, rows), BF16),
        pltpu.VMEM((count, WIDE), F32),
        pltpu.VMEM((2, count, LANES), F32),
        pltpu.VMEM((count, LANES), F32),
        dma((9,)),
        dma((4,)),
        dma((4,)),
        dma((1,)),
        dma((CHUNKS,)),
        dma((1,)),
        dma((lane_of(GATHER, CHUNKS, 0),)),
        dma((1,)),
        dma((lane_of(REDUCE, CHUNKS, 0),)),
        dma((1,)),
        dma((CHUNKS,)),
    ]
    return pl.pallas_call(
        functools.partial(kernel, n_tok),
        out_shape=jax.ShapeDtypeStruct(tokens.shape, BF16),
        in_specs=[hbm] * 9,
        out_specs=pl.BlockSpec(memory_space=pltpu.VMEM),
        scratch_shapes=scratch,
        compiler_params=pltpu.CompilerParams(
            collective_id=0, has_side_effects=True, vmem_limit_bytes=60 * 1024 * 1024
        ),
        cost_estimate=pl.CostEstimate(
            flops=4 * 2 * nz * CAP * D * units,
            bytes_accessed=4 * D * units,
            transcendentals=2 * nz * CAP * units,
        ),
    )(
        tokens,
        mod_shift[None, :],
        mod_scale[None, :],
        res_gate[None, :],
        routes.T,
        gate_fixed.T,
        expert_slot[None, :],
        weight_in,
        weight_out,
    )


def solution(mesh):
    placed = (
        P("tok", "place"),
        P(),
        P(),
        P(),
        P("tok", None, "place"),
        P("tok", "place", None),
        P(),
        P("tok", None),
        P("tok", None),
    )
    return jax.shard_map(
        shards, mesh=mesh, in_specs=placed, out_specs=P("tok", "place"), check_vma=False
    )
```
